32 devices in a mesh: ctx: 2 (over y), exp: 16 (over z, x, core).
Axes of the slice: x: 2, y: 2, z: 4, core: 2. Of those that a mesh axis runs over, the one named last changes fastest.
Arguments:
- queries: bfloat16 [256, 64, 576], P('ctx', 'exp'), may hold values from -16 to 16
- prior_codes: bfloat16 [768, 576], P('ctx'), may hold values from -4 to 4
- fresh_codes: bfloat16 [256, 576], P('ctx'), may hold values from -4 to 4
- prior_powers: int32 [6], P('ctx'), may hold values from -1 to 1
- fresh_powers: int32 [2], P('ctx'), may hold values from -1 to 1
- block_mask: int32 [2, 8], replicated, may hold values from 0 to 1, as said below
- value_up: bfloat16 [64, 512, 128], P('exp'), may hold values from -0.25 to 0.25
- output_weight: bfloat16 [8192, 7168], P('exp'), may hold values from -0.0625 to 0.0625
- residual: bfloat16 [256, 7168], P(('ctx', 'exp')), may hold values from -2 to 2
- norm_gain: bfloat16 [7168], replicated, may hold values from 0.5 to 1.5
- router: bfloat16 [7168, 16], replicated, may hold values from -0.0625 to 0.0625
- route_ids: int32 [256, 2], P(('ctx', 'exp')), may hold values from 0 to 15, all different within a row; in each aligned block of 8 rows (0 to 7, 8 to 15, ...) at most 2 rows name the same one
- gate_weight: bfloat16 [16, 7168, 2048], P('exp', None, 'ctx'), may hold values from -0.0625 to 0.0625
- up_weight: bfloat16 [16, 7168, 2048], P('exp', None, 'ctx'), may hold values from -0.0625 to 0.0625
- down_weight: bfloat16 [16, 2048, 7168], P('exp', 'ctx'), may hold values from -0.125 to 0.125
Outputs:
- layer_out: bfloat16 [256, 7168], P(('ctx', 'exp'))
The draws below stay inside these ranges and needn't reach their ends.
Inputs may be any that keep to these rules, and one draw needn't show every extreme that they name: block_mask[q, k] is 1 exactly when key block k (the prior blocks first, then the new ones) lies in the same document as new block q and not after it; every new block sees itself. `route_ids`: the 8 tokens of one device name one expert at most 2 times in all.
All inputs are finite; a program needn't handle non-finite values.
Results may differ from the reference program's by a relative error of at most 0.034.
Values may be sent and summed in bfloat16 or wider, within the bound.
A program may use at most 128 MiB of HBM per device.

```python
import math
import jax
import jax.numpy as jnp
import numpy as np
from jax import lax

D = 7168
LATENT = 512
ROPE = 64
NOPE = 128
VHEAD = 128
FF = 2048
HEAD_DEV = 4
ROUTES = 2
TOK_DEV = 8
PB = 3
HEADS = 64
EXPERTS = 16
CAP = 2
FRESH = 256
PRIOR = 768
N_CTX = 2
N_EXP = 16


def shared_codes(key, reach):
    raw = jax.random.normal(key, (TOK_DEV * N_EXP * N_CTX, LATENT + ROPE), jnp.float32)
    return jnp.clip(raw, -reach, reach)


def draw_fresh_codes(key, part):
    code_rows = shared_codes(key, 4.0)
    return code_rows.astype(jnp.bfloat16)


def draw_queries(key, part):
    shape = (TOK_DEV * N_EXP * N_CTX, HEAD_DEV * N_EXP, LATENT + ROPE)
    key = jax.random.fold_in(key, 7)
    result = jnp.clip(jax.random.normal(key, shape, jnp.float32), -4.0, 4.0)
    return result.astype(jnp.bfloat16)


def draw_prior_powers(key, part):
    key = jax.random.fold_in(key, 13)
    first_key, second_key = jax.random.split(key)
    count = PB * N_CTX
    values = jax.random.randint(first_key, (count,), -1, 2)
    step = jax.random.randint(second_key, (), 1, 3)
    other = (values[count - 1] + 1 + step) % 3 - 1
    return values.at[0].set(other).astype(jnp.int32)


def draw_block_mask(key, part):
    key = jax.random.fold_in(key, 5)
    first_key, second_key = jax.random.split(key)
    block_total = (PB + 1) * N_CTX
    first_new = PB * N_CTX
    start_block = jax.random.randint(first_key, (), 0, first_new + 1)
    fresh_starts = jax.random.randint(second_key, (block_total,), 0, 2)
    key_block = jnp.arange(block_total)
    starts = jnp.where(key_block == start_block, 1, jnp.where(key_block > first_new, fresh_starts, 0))
    document = jnp.cumsum(starts)
    query_block = first_new + jnp.arange(N_CTX)
    same_doc = document[None, :] == document[query_block][:, None]
    return jnp.logical_and(same_doc, key_block[None, :] <= query_block[:, None]).astype(jnp.int32)


def levels(stream_key, dims, cuts, smallest, high):
    level = 1.0
    for dim, shards_of in cuts:
        heights = jax.random.uniform(jax.random.fold_in(jax.random.fold_in(stream_key, 6), dim), (shards_of,), jnp.float32, smallest / len(cuts), high / len(cuts))
        level = level * jnp.repeat(jnp.exp(heights), dims[dim] // shards_of).reshape((-1,) + (1,) * (len(dims) - 1 - dim))
    return level


def deal_out(rng, own, number, rows, count, top, limit, lean):
    order = jax.random.permutation(rng, count)
    crowded, ordinary = load_shares(count, rows * top, limit, lean, True), load_shares(count, rows * top, limit, lean, False)
    places = jnp.arange(count)

    def named(lengths, turn):
        used = int((lengths > 0).sum())
        fixed = max(1, used // 4)
        passed = fixed + (places - fixed + turn * (used - fixed)) % max(1, count - fixed)
        return jnp.zeros((count,), jnp.int32).at[order[jnp.where(places < fixed, places, passed)]].set(jnp.asarray(lengths, jnp.int32))

    lengths = jnp.where(number % 4 == 0, named(crowded, number // 4), named(ordinary, number - number // 4 - 1))
    mixed = jax.random.permutation(jax.random.fold_in(own, 3), count)
    source_of, receiver = mixed[0:count // 2 * 2:2], mixed[1:count // 2 * 2:2]
    slack = jnp.minimum(lengths[source_of] - 1, limit - lengths[receiver]) // 2
    slack = jnp.where((source_of == order[0]) | (receiver == order[0]) | (lengths[receiver] == 0), 0, jnp.maximum(slack, 0))
    passed = jax.random.randint(jax.random.fold_in(own, 4), (count // 2,), 0, 1 << 20) % (slack + 1)
    lengths = lengths.at[source_of].add(-passed).at[receiver].add(passed)
    labels = jnp.searchsorted(jnp.cumsum(lengths), jnp.arange(rows * top), side="right").astype(jnp.int32)
    grid = labels.reshape(top, rows).T
    grid = grid[jax.random.permutation(jax.random.fold_in(own, 1), rows)]
    turn = jax.random.randint(jax.random.fold_in(own, 2), (rows, 1), 0, top)
    return jnp.take_along_axis(grid, (jnp.arange(top)[None, :] + turn) % top, axis=1)


def load_shares(number_of, total, most, skew, full):
    portions = [(1 << 20) // math.isqrt(grade ** skew) + 1 for grade in range(1, number_of + 1)]
    largest = most if full else min(most, max(-(-total // number_of), total * portions[0] // sum(portions)))
    least = 1 if total - largest >= number_of - 1 else 0
    counts, spare = [largest] + [least] * (number_of - 1), total - largest - least * (number_of - 1)
    while spare > 0:
        candidates = [i for i in range(1, number_of) if counts[i] < largest] or [i for i in range(1, number_of) if counts[i] < most]
        pool, remaining = sum([portions[i] for i in candidates]), spare
        for i in candidates:
            addition = min(most - counts[i], max(1, remaining * portions[i] // pool), spare)
            counts[i] = counts[i] + addition
            spare = spare - addition
    return np.array(counts)


def centred(own_key, extent, width, bound, pieces=(), held_as=jnp.bfloat16):
    values = jax.random.normal(own_key, extent, jnp.float32) * width
    if len(pieces) > 0:
        values = levels(own_key, extent, pieces, -0.22, 0.18) * values
    return jnp.clip(values, min=-bound, max=bound).astype(held_as)


def setup_inputs(seed: int = 0) -> dict:
    seeds = jax.random.split(jax.random.key(seed), 16)
    queries = draw_queries(jax.random.fold_in(seeds[15], 71), 0)
    prior_codes = centred(seeds[1], (PRIOR, LATENT + ROPE), 1.0, 4.0, ((0, 2),))
    fresh_codes = draw_fresh_codes(jax.random.fold_in(seeds[15], 71), 0)
    prior_powers = draw_prior_powers(jax.random.fold_in(seeds[15], 71), 0)
    fresh_powers = jax.random.randint(seeds[4], (N_CTX,), -1, 2).astype(jnp.int32)
    block_mask = draw_block_mask(jax.random.fold_in(seeds[15], 71), 0)
    value_up = centred(seeds[6], (HEADS, LATENT, VHEAD), LATENT ** -0.5, 0.25, ((0, 16),))
    output_weight = centred(seeds[7], (HEADS * VHEAD, D), (HEADS * VHEAD) ** -0.5, 0.0625, ((0, 16),))
    residual = centred(seeds[8], (FRESH, D), 0.3, 2.0, ((0, 32),))
    norm_gain = jnp.clip(1.0 + 0.1 * jax.random.normal(seeds[9], (D,), jnp.float32), 0.5, 1.5).astype(jnp.bfloat16)
    router = centred(seeds[10], (D, EXPERTS), D ** -0.5, 0.0625)
    route_ids_keys = jax.random.split(jax.random.fold_in(seeds[11], 1), FRESH // TOK_DEV)
    route_ids_turns = jax.random.permutation(jax.random.fold_in(seeds[11], 3), FRESH // TOK_DEV)
    route_ids = jax.vmap(lambda own, number: deal_out(jax.random.fold_in(seeds[11], 2), own, number, TOK_DEV, EXPERTS, ROUTES, CAP, 2))(route_ids_keys, route_ids_turns).reshape((FRESH, ROUTES))
    gate_weight = centred(seeds[12], (EXPERTS, D, FF), D ** -0.5, 0.0625, ((0, 16), (2, 2)))
    up_weight = centred(seeds[13], (EXPERTS, D, FF), D ** -0.5, 0.0625, ((0, 16), (2, 2)))
    down_weight = centred(seeds[14], (EXPERTS, FF, D), FF ** -0.5, 0.125, ((0, 16), (1, 2)))
    return {"queries": queries, "prior_codes": prior_codes, "fresh_codes": fresh_codes, "prior_powers": prior_powers, "fresh_powers": fresh_powers, "block_mask": block_mask, "value_up": value_up, "output_weight": output_weight, "residual": residual, "norm_gain": norm_gain, "router": router, "route_ids": route_ids, "gate_weight": gate_weight, "up_weight": up_weight, "down_weight": down_weight}


def power_two(powers):
    return jnp.where(powers < 0, 0.5, jnp.where(powers > 0, 2.0, 1.0)).astype(jnp.float32)

def reference(queries, prior_codes, fresh_codes, prior_powers, fresh_powers, block_mask, value_up, output_weight, residual, norm_gain, router, route_ids, gate_weight, up_weight, down_weight):
    rows_block = TOK_DEV * N_EXP
    fresh_total = rows_block * N_CTX
    prior_total = PB * rows_block * N_CTX
    key_total = prior_total + fresh_total
    prior_scale = jnp.repeat(power_two(prior_powers), rows_block)
    fresh_scale = jnp.repeat(power_two(fresh_powers), rows_block)
    latent = jnp.concatenate([prior_codes.astype(jnp.float32) * prior_scale[:, None], fresh_codes.astype(jnp.float32) * fresh_scale[:, None]], axis=0).astype(jnp.bfloat16)
    query_block = jnp.arange(fresh_total) // rows_block
    key_block = jnp.arange(key_total) // rows_block
    allowed = block_mask[query_block[:, None], key_block[None, :]] > 0
    allowed = jnp.logical_and(allowed, jnp.arange(key_total)[None, :] <= prior_total + jnp.arange(fresh_total)[:, None])
    scale_factor = 1.0 / (NOPE + ROPE) ** 0.5

    def one_head(head_index):
        head_queries = queries[:, head_index, :]
        scores = jnp.dot(head_queries, latent.T, preferred_element_type=jnp.float32) * scale_factor
        scores = jnp.where(allowed, scores, -1e+30)
        row_top = lax.optimization_barrier(jnp.max(scores, axis=1, keepdims=True))
        weights = jnp.where(allowed, jnp.exp(scores - row_top), 0.0)
        row_total = lax.optimization_barrier(jnp.sum(weights, axis=1, keepdims=True))
        mixture = jnp.dot(weights.astype(jnp.bfloat16), latent[:, :LATENT], preferred_element_type=jnp.float32)
        attended = (mixture / row_total).astype(jnp.bfloat16)
        return jnp.dot(attended, value_up[head_index], preferred_element_type=jnp.float32).astype(jnp.bfloat16)
    heads_out = lax.map(one_head, jnp.arange(HEADS))
    head_dev = HEADS // N_EXP
    grouped = heads_out.reshape(N_EXP, head_dev, fresh_total, VHEAD).transpose(0, 2, 1, 3).reshape(N_EXP, fresh_total, head_dev * VHEAD)
    out_groups = output_weight.reshape(N_EXP, head_dev * VHEAD, D)

    def group_step(running, pair):
        group_rows, group_weight = pair
        rounded = jnp.dot(group_rows, group_weight, preferred_element_type=jnp.float32).astype(jnp.bfloat16)
        rounded = lax.optimization_barrier(rounded)
        return (running + rounded.astype(jnp.float32), None)
    attention, unused = lax.scan(group_step, jnp.zeros((fresh_total, D), jnp.float32), (grouped, out_groups))
    hidden = (residual.astype(jnp.float32) + attention).astype(jnp.bfloat16)
    hidden_wide = hidden.astype(jnp.float32)
    normed = (hidden_wide * lax.rsqrt(lax.optimization_barrier(jnp.mean(hidden_wide * hidden_wide, axis=1, keepdims=True)) + 1e-06) * norm_gain.astype(jnp.float32)).astype(jnp.bfloat16)
    affinity = jax.nn.sigmoid(jnp.dot(normed, router, preferred_element_type=jnp.float32))
    route_hits = route_ids[:, :, None] == jnp.arange(EXPERTS)[None, None, :]
    chosen = lax.optimization_barrier(jnp.sum(jnp.where(route_hits, affinity[:, None, :], 0.0), axis=2))
    gate_values = 2.5 * chosen / lax.optimization_barrier(jnp.sum(chosen, axis=1, keepdims=True))
    devices = N_CTX * N_EXP
    flat_ids = route_ids.reshape(devices, TOK_DEV * ROUTES)
    flat_hits = (flat_ids[:, :, None] == jnp.arange(EXPERTS)[None, None, :]).astype(jnp.int32)
    before = jnp.cumsum(flat_hits, axis=1) - flat_hits
    slot_index = lax.optimization_barrier(jnp.sum(before * flat_hits, axis=2))
    source = jnp.arange(devices)[:, None]
    position = (source * CAP + slot_index).astype(jnp.int32)
    token_of = (source * TOK_DEV + jnp.arange(TOK_DEV * ROUTES)[None, :] // ROUTES).astype(jnp.int32)
    slot_table = jnp.zeros((EXPERTS, devices * CAP), jnp.int32).at[flat_ids, position].set(token_of)
    slice_width = FF // N_CTX

    def one_expert(expert_index):
        token_rows = normed[slot_table[expert_index]]
        gate_proj = jnp.dot(token_rows, gate_weight[expert_index], preferred_element_type=jnp.float32)
        up_proj = jnp.dot(token_rows, up_weight[expert_index], preferred_element_type=jnp.float32)
        inner_act = (jax.nn.silu(gate_proj) * up_proj).astype(jnp.bfloat16)
        slice_acts = inner_act.reshape(-1, N_CTX, slice_width).transpose(1, 0, 2).astype(jnp.float32)
        down_slices = down_weight[expert_index].reshape(N_CTX, slice_width, D).astype(jnp.float32)
        slice_out = jnp.einsum('cnf,cfd->cnd', slice_acts, down_slices).astype(jnp.bfloat16)
        slice_out = lax.optimization_barrier(slice_out)
        return lax.optimization_barrier(jnp.sum(slice_out.astype(jnp.float32), axis=0)).astype(jnp.bfloat16)
    expert_out = lax.map(one_expert, jnp.arange(EXPERTS))
    routed = expert_out[flat_ids, position].reshape(fresh_total, ROUTES, D).astype(jnp.float32)
    expert_mix = lax.optimization_barrier(jnp.sum(gate_values[:, :, None] * routed, axis=1))
    return (hidden_wide + expert_mix).astype(jnp.bfloat16)
```

```python
import functools

import jax
import jax.numpy as jnp
from jax import lax
from jax.experimental import pallas as pl
from jax.experimental.pallas import tpu as pltpu
from jax.sharding import PartitionSpec as P

ROPE = 64
NOPE = 128
MESH = pl.DeviceIdType.MESH
CHUNKS = 4
PIECES = 8


def power_two(powers):
    return jnp.where(powers < 0, 0.5, jnp.where(powers > 0, 2.0, 1.0)).astype(jnp.float32)


def greet(peers):
    barrier = pltpu.get_barrier_semaphore()
    for peer in peers:
        pl.semaphore_signal(barrier, inc=1, device_id=peer, device_id_type=MESH)
    pl.semaphore_wait(barrier, len(peers))


def attention_kernel(
    ctx_count,
    exp_count,
    q_ref,
    lat_ref,
    mask_ref,
    up_ref,
    w_hbm,
    out_ref,
    keys,
    flat,
    w_buf,
    *rest,
):
    stages = exp_count.bit_length() - 1
    held = rest[:stages]
    landed = rest[stages : 2 * stages]
    w_sem, lat_send, lat_recv, fwd_send, fwd_recv, rs_send, rs_recv = rest[2 * stages :]
    ctx = lax.axis_index("ctx")
    exp = lax.axis_index("exp")
    heads, latent_width, vhead = up_ref.shape
    rows = q_ref.shape[0] // heads
    key_width, key_rows = lat_ref.shape
    half = key_width // 2
    model = out_ref.shape[1]
    side = model // 2
    width = side // CHUNKS
    bits = [lax.rem(exp // (1 << i), 2) for i in range(stages)]
    partners = [exp + (1 - 2 * bits[i]) * (1 << i) for i in range(stages)]

    weights_in = []
    for chunk in range(CHUNKS):
        pair = []
        for h in range(2):
            columns = pl.ds(h * side + chunk * width, width)
            copy = pltpu.make_async_copy(
                w_hbm.at[:, columns], w_buf.at[:, columns], w_sem.at[chunk, h]
            )
            copy.start()
            pair.append(copy)
        weights_in.append(pair)

    others = [lax.rem(ctx + d, ctx_count) for d in range(1, ctx_count)]
    senders = [lax.rem(ctx + ctx_count - d, ctx_count) for d in range(1, ctx_count)]
    greet([(o, exp) for o in others] + [(ctx, p) for p in partners])

    part = pl.ds(pl.multiple_of(bits[0] * half, half), half)
    sends = []
    for d, other in enumerate(others):
        copy = pltpu.make_async_remote_copy(
            src_ref=lat_ref.at[part],
            dst_ref=keys.at[ctx, part],
            send_sem=lat_send.at[d],
            recv_sem=lat_recv.at[d],
            device_id=(other, exp),
            device_id_type=MESH,
        )
        copy.start()
        sends.append(copy)
    keys[ctx] = lat_ref[...]
    forwards = []
    for d, sender in enumerate(senders):
        sends[d].wait_recv()
        copy = pltpu.make_async_remote_copy(
            src_ref=keys.at[sender, part],
            dst_ref=keys.at[sender, part],
            send_sem=fwd_send.at[d],
            recv_sem=fwd_recv.at[d],
            device_id=(ctx, partners[0]),
            device_id_type=MESH,
        )
        copy.start()
        forwards.append(copy)
    for copy in forwards:
        copy.wait_recv()

    factor = 1.0 / (NOPE + ROPE) ** 0.5
    for h in range(heads):
        q_head = q_ref[h * rows : (h + 1) * rows, :]
        scores = []
        for o in range(ctx_count):
            raw = jnp.dot(q_head, keys[o], preferred_element_type=jnp.float32) * factor
            live = mask_ref[:, o * key_rows : (o + 1) * key_rows] > 0
            scores.append(jnp.where(live, raw, -1e30))
        top = jnp.max(scores[0], axis=1, keepdims=True)
        for s in scores[1:]:
            top = jnp.maximum(top, jnp.max(s, axis=1, keepdims=True))
        total = jnp.zeros((rows, 1), jnp.float32)
        mixture = jnp.zeros((rows, latent_width), jnp.float32)
        for o in range(ctx_count):
            live = mask_ref[:, o * key_rows : (o + 1) * key_rows] > 0
            weights = jnp.where(live, jnp.exp(scores[o] - top), 0.0)
            total = total + jnp.sum(weights, axis=1, keepdims=True)
            mixture = mixture + lax.dot_general(
                weights.astype(jnp.bfloat16),
                keys[o, :latent_width, :],
                (((1,), (1,)), ((), ())),
                preferred_element_type=jnp.float32,
            )
        attended = (mixture / total).astype(jnp.bfloat16)
        head_out = jnp.dot(attended, up_ref[h], preferred_element_type=jnp.float32)
        flat[:, h * vhead : (h + 1) * vhead] = head_out.astype(jnp.bfloat16)

    tokens = rows // exp_count

    def exchange(stage, chunk):
        return pltpu.make_async_remote_copy(
            src_ref=held[stage].at[chunk, :, 1 - bits[stage]],
            dst_ref=landed[stage].at[chunk],
            send_sem=rs_send.at[stage, chunk],
            recv_sem=rs_recv.at[stage, chunk],
            device_id=(ctx, partners[stage]),
            device_id_type=MESH,
        )

    for turn in range(CHUNKS + stages):
        if turn < CHUNKS:
            sides = []
            for h in range(2):
                weights_in[turn][h].wait()
                at = h * side + turn * width
                term = jnp.dot(
                    flat[...], w_buf[:, at : at + width], preferred_element_type=jnp.float32
                )
                sides.append(term.reshape(exp_count, tokens, width))
            both = jnp.concatenate(sides, axis=1).astype(jnp.bfloat16)
            held[0][turn] = both.reshape(exp_count // 2, 2, 2 * tokens, width)
            exchange(0, turn).start()
        for stage in reversed(range(stages)):
            chunk = turn - 1 - stage
            if chunk < 0 or chunk >= CHUNKS:
                continue
            exchange(stage, chunk).wait_recv()
            mine = held[stage][chunk, :, pl.ds(bits[stage], 1)]
            count = mine.shape[0]
            summed = mine.reshape(count, 2 * tokens, width).astype(jnp.float32)
            summed = summed + landed[stage][chunk].astype(jnp.float32)
            if stage + 1 < stages:
                held[stage + 1][chunk] = summed.astype(jnp.bfloat16).reshape(
                    count // 2, 2, 2 * tokens, width
                )
                exchange(stage + 1, chunk).start()
            else:
                last = summed.reshape(2 * tokens, width)
                for h in range(2):
                    at = h * side + chunk * width
                    out_ref[:, at : at + width] = last[h * tokens : (h + 1) * tokens, :]
    for d in range(ctx_count - 1):
        sends[d].wait_send()
        forwards[d].wait_send()
    for stage in range(stages):
        for chunk in range(CHUNKS):
            exchange(stage, chunk).wait_send()


def attention_call(ctx_count, exp_count, q_rows, latent_t, mask, value_up, output_weight):
    heads, latent_width, vhead = value_up.shape
    rows = q_rows.shape[0] // heads
    key_width, key_rows = latent_t.shape
    model = output_weight.shape[1]
    tokens = rows // exp_count
    stages = exp_count.bit_length() - 1
    width = model // 2 // CHUNKS
    vmem = pl.BlockSpec(memory_space=pltpu.VMEM)
    scratch = [
        pltpu.VMEM((ctx_count, key_width, key_rows), jnp.bfloat16),
        pltpu.VMEM((rows, heads * vhead), jnp.bfloat16),
        pltpu.VMEM(output_weight.shape, jnp.bfloat16),
    ]
    for stage in range(stages):
        blocks = exp_count >> (stage + 1)
        scratch.append(pltpu.VMEM((CHUNKS, blocks, 2, 2 * tokens, width), jnp.bfloat16))
    for stage in range(stages):
        blocks = exp_count >> (stage + 1)
        scratch.append(pltpu.VMEM((CHUNKS, blocks, 2 * tokens, width), jnp.bfloat16))
    dma = pltpu.SemaphoreType.DMA
    scratch += [
        dma((CHUNKS, 2)),
        dma((ctx_count - 1,)),
        dma((ctx_count - 1,)),
        dma((ctx_count - 1,)),
        dma((ctx_count - 1,)),
        dma((stages, CHUNKS)),
        dma((stages, CHUNKS)),
    ]
    return pl.pallas_call(
        functools.partial(attention_kernel, ctx_count, exp_count),
        out_shape=jax.ShapeDtypeStruct((tokens, model), jnp.float32),
        in_specs=[vmem, vmem, vmem, vmem, pl.BlockSpec(memory_space=pl.ANY)],
        out_specs=vmem,
        scratch_shapes=scratch,
        compiler_params=pltpu.CompilerParams(
            collective_id=0, has_side_effects=True, vmem_limit_bytes=48 << 20
        ),
    )(q_rows, latent_t, mask, value_up, output_weight)


def expert_kernel(
    ctx_count,
    exp_count,
    buf_ref,
    gate_hbm,
    up_hbm,
    down_hbm,
    out_ref,
    gate_w,
    up_w,
    down_w,
    recv,
    rows_in,
    ret_in,
    out_buf,
    w_sem,
    d_send,
    d_recv,
    f_send,
    f_recv,
    r_send,
    r_recv,
    b_send,
    b_recv,
):
    ctx = lax.axis_index("ctx")
    exp = lax.axis_index("exp")
    width = buf_ref.shape[2]
    block = buf_ref.shape[1]
    slots = exp_count * block // PIECES
    weights_in = []
    for which, (source, target) in enumerate(((gate_hbm, gate_w), (up_hbm, up_w))):
        for piece in range(PIECES):
            span = pl.ds(piece * width, width)
            weights_in.append(
                pltpu.make_async_copy(
                    source.at[0, span], target.at[span], w_sem.at[which, piece]
                )
            )
    for piece in range(PIECES):
        span = pl.ds(piece * width, width)
        weights_in.append(
            pltpu.make_async_copy(
                down_hbm.at[0, :, span], down_w.at[:, span], w_sem.at[2, piece]
            )
        )
    for copy in weights_in:
        copy.start()

    order = sorted(range(1, exp_count), key=lambda k: abs(k - exp_count // 2))
    to = {k: lax.rem(exp + k, exp_count) for k in range(exp_count)}
    origin = {k: lax.rem(exp + exp_count - k, exp_count) for k in range(exp_count)}
    others = [lax.rem(ctx + d, ctx_count) for d in range(1, ctx_count)]
    senders = [lax.rem(ctx + ctx_count - d, ctx_count) for d in range(1, ctx_count)]
    greet([(ctx, to[k]) for k in order] + [(o, exp) for o in others])

    def dispatch(k):
        return pltpu.make_async_remote_copy(
            src_ref=buf_ref.at[to[k]],
            dst_ref=recv.at[ctx, exp],
            send_sem=d_send.at[k],
            recv_sem=d_recv.at[k],
            device_id=(ctx, to[k]),
            device_id_type=MESH,
        )

    def forward(d, k):
        return pltpu.make_async_remote_copy(
            src_ref=recv.at[ctx, origin[k]],
            dst_ref=recv.at[ctx, origin[k]],
            send_sem=f_send.at[d, k],
            recv_sem=f_recv.at[d, k],
            device_id=(others[d], exp),
            device_id_type=MESH,
        )

    def give_back(d, k):
        return pltpu.make_async_remote_copy(
            src_ref=recv.at[others[d], to[k]],
            dst_ref=ret_in.at[d, to[k]],
            send_sem=r_send.at[d, k],
            recv_sem=r_recv.at[d, k],
            device_id=(others[d], exp),
            device_id_type=MESH,
        )

    def hand_in(k):
        return pltpu.make_async_remote_copy(
            src_ref=out_buf.at[to[k]],
            dst_ref=out_ref.at[exp],
            send_sem=b_send.at[k],
            recv_sem=b_recv.at[k],
            device_id=(ctx, to[k]),
            device_id_type=MESH,
        )

    for k in order:
        dispatch(k).start()
    recv[ctx, exp] = buf_ref[exp]
    for d in range(ctx_count - 1):
        forward(d, 0).start()
    arrival = sorted(range(1, exp_count), key=lambda k: min(k, exp_count - k))
    for k in arrival:
        dispatch(k).wait_recv()
        for d in range(ctx_count - 1):
            forward(d, k).start()

    row = lax.broadcasted_iota(jnp.int32, (exp_count * block, exp_count * block), 0)
    column = lax.broadcasted_iota(jnp.int32, (exp_count * block, exp_count * block), 1)
    split = jnp.where(
        column == lax.rem(row, slots) * PIECES + row // slots, 1.0, 0.0
    ).astype(jnp.bfloat16)
    merge = jnp.where(
        row == lax.rem(column, slots) * PIECES + column // slots, 1.0, 0.0
    ).astype(jnp.bfloat16)

    def spread(which):
        packed = recv[which].reshape(exp_count * block, width)
        apart = jnp.dot(split, packed, preferred_element_type=jnp.float32).astype(jnp.bfloat16)
        at = pl.ds(pl.multiple_of(which * slots, slots), slots)
        for piece in range(PIECES):
            rows_in[piece, at, :] = apart[piece * slots : (piece + 1) * slots, :]

    spread(ctx)
    for d in range(ctx_count - 1):
        for k in [0] + arrival:
            forward(d, k).wait_recv()
        spread(senders[d])

    gate = None
    up = None
    for piece in range(PIECES):
        weights_in[piece].wait()
        weights_in[PIECES + piece].wait()
        span = slice(piece * width, (piece + 1) * width)
        rows = rows_in[piece]
        gate_part = jnp.dot(rows, gate_w[span, :], preferred_element_type=jnp.float32)
        up_part = jnp.dot(rows, up_w[span, :], preferred_element_type=jnp.float32)
        gate = gate_part if gate is None else gate + gate_part
        up = up_part if up is None else up + up_part
    inner = (gate / (1.0 + jnp.exp(-gate)) * up).astype(jnp.bfloat16)
    for piece in range(PIECES):
        weights_in[2 * PIECES + piece].wait()
        span = slice(piece * width, (piece + 1) * width)
        result = jnp.dot(inner, down_w[:, span], preferred_element_type=jnp.float32)
        rows_in[piece] = result.astype(jnp.bfloat16)

    for k in order:
        dispatch(k).wait_send()
    for d in range(ctx_count - 1):
        for k in range(exp_count):
            forward(d, k).wait_send()

    def gather(which):
        at = pl.ds(pl.multiple_of(which * slots, slots), slots)
        apart = jnp.concatenate([rows_in[piece, at, :] for piece in range(PIECES)], axis=0)
        packed = jnp.dot(merge, apart, preferred_element_type=jnp.float32).astype(jnp.bfloat16)
        recv[which] = packed.reshape(exp_count, block, width)

    for d in range(ctx_count - 1):
        gather(others[d])
        for k in order + [0]:
            give_back(d, k).start()
    gather(ctx)
    for k in order + [0]:
        total = recv[ctx, to[k]].astype(jnp.float32)
        for d in range(ctx_count - 1):
            give_back(d, k).wait_recv()
            total = total + ret_in[d, to[k]].astype(jnp.float32)
        if k == 0:
            out_ref[exp] = total.astype(jnp.bfloat16)
        else:
            out_buf[to[k]] = total.astype(jnp.bfloat16)
            hand_in(k).start()
    for k in order:
        hand_in(k).wait_recv()
    for k in order:
        hand_in(k).wait_send()
    for d in range(ctx_count - 1):
        for k in range(exp_count):
            give_back(d, k).wait_send()


def expert_call(ctx_count, exp_count, buffer, gate_weight, up_weight, down_weight):
    block, width = buffer.shape[1:]
    model, hidden = gate_weight.shape[1:]
    slots = exp_count * block // PIECES
    vmem = pl.BlockSpec(memory_space=pltpu.VMEM)
    anywhere = pl.BlockSpec(memory_space=pl.ANY)
    dma = pltpu.SemaphoreType.DMA
    return pl.pallas_call(
        functools.partial(expert_kernel, ctx_count, exp_count),
        out_shape=jax.ShapeDtypeStruct(buffer.shape, jnp.bfloat16),
        in_specs=[vmem, anywhere, anywhere, anywhere],
        out_specs=vmem,
        scratch_shapes=[
            pltpu.VMEM((model, hidden), jnp.bfloat16),
            pltpu.VMEM((model, hidden), jnp.bfloat16),
            pltpu.VMEM((hidden, model), jnp.bfloat16),
            pltpu.VMEM((ctx_count, exp_count, block, width), jnp.bfloat16),
            pltpu.VMEM((PIECES, ctx_count * slots, width), jnp.bfloat16),
            pltpu.VMEM((ctx_count - 1, exp_count, block, width), jnp.bfloat16),
            pltpu.VMEM((exp_count, block, width), jnp.bfloat16),
            dma((3, PIECES)),
            dma((exp_count,)),
            dma((exp_count,)),
            dma((ctx_count - 1, exp_count)),
            dma((ctx_count - 1, exp_count)),
            dma((ctx_count - 1, exp_count)),
            dma((ctx_count - 1, exp_count)),
            dma((exp_count,)),
            dma((exp_count,)),
        ],
        compiler_params=pltpu.CompilerParams(
            collective_id=1, has_side_effects=True, vmem_limit_bytes=62 << 20
        ),
    )(buffer, gate_weight, up_weight, down_weight)


def on_device(
    queries,
    prior_codes,
    fresh_codes,
    prior_powers,
    fresh_powers,
    block_mask,
    value_up,
    output_weight,
    residual,
    norm_gain,
    router,
    route_ids,
    gate_weight,
    up_weight,
    down_weight,
):
    ctx_count = lax.axis_size("ctx")
    exp_count = lax.axis_size("exp")
    ctx_index = lax.axis_index("ctx")
    rows_block, head_count, key_width = queries.shape
    prior_blocks = prior_powers.shape[0]
    own_blocks = prior_blocks + 1
    scales = power_two(jnp.concatenate([prior_powers, fresh_powers], axis=0))
    code_rows = jnp.concatenate([prior_codes, fresh_codes], axis=0)
    latent_t = (
        code_rows.T.astype(jnp.float32) * jnp.repeat(scales, rows_block)[None, :]
    ).astype(jnp.bfloat16)
    q_rows = queries.transpose(1, 0, 2).reshape(head_count * rows_block, key_width)

    mask_row = lax.dynamic_index_in_dim(block_mask, ctx_index, 0, keepdims=False)
    prior_mask = mask_row[: prior_blocks * ctx_count].reshape(ctx_count, prior_blocks)
    fresh_mask = mask_row[prior_blocks * ctx_count :].reshape(ctx_count, 1)
    live = jnp.concatenate([prior_mask, fresh_mask], axis=1) > 0
    position = jnp.arange(rows_block)
    is_fresh = jnp.arange(own_blocks)[None, :] == prior_blocks
    is_own = jnp.arange(ctx_count)[:, None] == ctx_index
    diagonal = jnp.logical_and(is_fresh, is_own)
    causal = position[:, None] >= position[None, :]
    later = jnp.logical_and(is_fresh, jnp.arange(ctx_count)[:, None] > ctx_index)
    live = jnp.logical_and(live, jnp.logical_not(later))
    allowed = jnp.logical_and(
        live[None, :, :, None],
        jnp.logical_or(jnp.logical_not(diagonal)[None, :, :, None], causal[:, None, None, :]),
    )
    mask = allowed.reshape(rows_block, ctx_count * own_blocks * rows_block).astype(jnp.float32)

    attention = attention_call(
        ctx_count, exp_count, q_rows, latent_t, mask, value_up, output_weight
    )
    hidden = (residual.astype(jnp.float32) + attention).astype(jnp.bfloat16)
    hidden_wide = hidden.astype(jnp.float32)
    normed = (
        hidden_wide
        * lax.rsqrt(jnp.mean(hidden_wide * hidden_wide, axis=1, keepdims=True) + 1e-06)
        * norm_gain.astype(jnp.float32)
    ).astype(jnp.bfloat16)
    expert_count = router.shape[1]
    token_count, route_count = route_ids.shape
    model_width = normed.shape[1]
    capacity = token_count * route_count * 2 // expert_count
    affinity = jax.nn.sigmoid(jnp.dot(normed, router, preferred_element_type=jnp.float32))
    route_hits = route_ids[:, :, None] == jnp.arange(expert_count)[None, None, :]
    chosen = jnp.sum(jnp.where(route_hits, affinity[:, None, :], 0.0), axis=2)
    gate_values = 2.5 * chosen / jnp.sum(chosen, axis=1, keepdims=True)
    flat_hits = route_hits.reshape(token_count * route_count, expert_count).astype(jnp.int32)
    before = jnp.cumsum(flat_hits, axis=0) - flat_hits
    slot_index = jnp.sum(before * flat_hits, axis=1)
    target = route_ids.reshape(-1) * capacity + slot_index
    placing = (target[None, :] == jnp.arange(expert_count * capacity)[:, None]).astype(jnp.bfloat16)
    to_token = jnp.sum(placing.reshape(-1, token_count, route_count), axis=2)
    buffer = jnp.dot(to_token, normed, preferred_element_type=jnp.float32).astype(jnp.bfloat16)
    summed = expert_call(
        ctx_count,
        exp_count,
        buffer.reshape(expert_count, capacity * PIECES, model_width // PIECES),
        gate_weight,
        up_weight,
        down_weight,
    ).reshape(expert_count * capacity, model_width)
    gathered_back = jnp.dot(
        jnp.transpose(placing), summed, preferred_element_type=jnp.float32
    ).reshape(token_count, route_count, model_width)
    expert_mix = jnp.sum(gate_values[:, :, None] * gathered_back, axis=1)
    return (hidden_wide + expert_mix).astype(jnp.bfloat16)


def solution(mesh):
    in_specs = (
        P("ctx", "exp", None),
        P("ctx", None),
        P("ctx", None),
        P("ctx"),
        P("ctx"),
        P(),
        P("exp", None, None),
        P("exp", None),
        P(("ctx", "exp"), None),
        P(),
        P(),
        P(("ctx", "exp"), None),
        P("exp", None, "ctx"),
        P("exp", None, "ctx"),
        P("exp", "ctx", None),
    )
    out_specs = P(("ctx", "exp"), None)
    return jax.shard_map(
        on_device, mesh=mesh, in_specs=in_specs, out_specs=out_specs, check_vma=False
    )
```

```python
import functools

import jax
import jax.numpy as jnp
from jax import lax
from jax.experimental import pallas as pl
from jax.experimental.pallas import tpu as pltpu
from jax.sharding import PartitionSpec as P

ROPE = 64
NOPE = 128
MESH = pl.DeviceIdType.MESH
CHUNKS = 4
PIECES = 8


def power_two(powers):
    return jnp.where(powers < 0, 0.5, jnp.where(powers > 0, 2.0, 1.0)).astype(jnp.float32)


def greet(peers):
    barrier = pltpu.get_barrier_semaphore()
    for peer in peers:
        pl.semaphore_signal(barrier, inc=1, device_id=peer, device_id_type=MESH)
    pl.semaphore_wait(barrier, len(peers))


def attention_kernel(
    ctx_count,
    exp_count,
    q_ref,
    lat_ref,
    mask_ref,
    up_ref,
    w_hbm,
    out_ref,
    keys,
    flat,
    w_buf,
    *rest,
):
    stages = exp_count.bit_length() - 1
    held = rest[:stages]
    landed = rest[stages : 2 * stages]
    w_sem, lat_send, lat_recv, fwd_send, fwd_recv, rs_send, rs_recv = rest[2 * stages :]
    ctx = lax.axis_index("ctx")
    exp = lax.axis_index("exp")
    heads, latent_width, vhead = up_ref.shape
    rows = q_ref.shape[0] // heads
    key_width, key_rows = lat_ref.shape
    half = key_width // 2
    model = out_ref.shape[1]
    side = model // 2
    width = side // CHUNKS
    bits = [lax.rem(exp // (1 << i), 2) for i in range(stages)]
    partners = [exp + (1 - 2 * bits[i]) * (1 << i) for i in range(stages)]

    others = [lax.rem(ctx + d, ctx_count) for d in range(1, ctx_count)]
    senders = [lax.rem(ctx + ctx_count - d, ctx_count) for d in range(1, ctx_count)]
    greet([(o, exp) for o in others] + [(ctx, p) for p in partners])

    part = pl.ds(pl.multiple_of(bits[0] * half, half), half)
    sends = []
    for d, other in enumerate(others):
        copy = pltpu.make_async_remote_copy(
            src_ref=lat_ref.at[part],
            dst_ref=keys.at[ctx, part],
            send_sem=lat_send.at[d],
            recv_sem=lat_recv.at[d],
            device_id=(other, exp),
            device_id_type=MESH,
        )
        copy.start()
        sends.append(copy)
    weights_in = []
    for chunk in range(CHUNKS):
        pair = []
        for h in range(2):
            columns = pl.ds(h * side + chunk * width, width)
            copy = pltpu.make_async_copy(
                w_hbm.at[:, columns], w_buf.at[:, columns], w_sem.at[chunk, h]
            )
            copy.start()
            pair.append(copy)
        weights_in.append(pair)


    factor = 1.0 / (NOPE + ROPE) ** 0.5

    def attend(h, key_block, live):
        q_head = q_ref[h * rows : (h + 1) * rows, :]
        raw = jnp.dot(q_head, key_block[...], preferred_element_type=jnp.float32) * factor
        raw = jnp.where(live, raw, -1e30)
        top = jnp.max(raw, axis=1, keepdims=True)
        weights = jnp.where(live, jnp.exp(raw - top), 0.0)
        total = jnp.sum(weights, axis=1, keepdims=True)
        mixture = lax.dot_general(
            weights.astype(jnp.bfloat16),
            key_block[:latent_width, :],
            (((1,), (1,)), ((), ())),
            preferred_element_type=jnp.float32,
        )
        return top, total, mixture

    live = mask_ref[ctx] > 0
    states = [attend(h, lat_ref, live) for h in range(heads)]
    forwards = []
    for d, sender in enumerate(senders):
        sends[d].wait_recv()
        copy = pltpu.make_async_remote_copy(
            src_ref=keys.at[sender, part],
            dst_ref=keys.at[sender, part],
            send_sem=fwd_send.at[d],
            recv_sem=fwd_recv.at[d],
            device_id=(ctx, partners[0]),
            device_id_type=MESH,
        )
        copy.start()
        forwards.append(copy)
    for d, sender in enumerate(senders):
        forwards[d].wait_recv()
        live = mask_ref[sender] > 0
        for h in range(heads):
            top, total, mixture = states[h]
            new_top, new_total, new_mixture = attend(h, keys.at[sender], live)
            both_top = jnp.maximum(top, new_top)
            shrink = jnp.exp(top - both_top)
            new_shrink = jnp.exp(new_top - both_top)
            states[h] = (
                both_top,
                total * shrink + new_total * new_shrink,
                mixture * shrink + new_mixture * new_shrink,
            )
    for h in range(heads):
        top, total, mixture = states[h]
        attended = (mixture / total).astype(jnp.bfloat16)
        head_out = jnp.dot(attended, up_ref[h], preferred_element_type=jnp.float32)
        flat[:, h * vhead : (h + 1) * vhead] = head_out.astype(jnp.bfloat16)

    tokens = rows // exp_count

    def exchange(stage, chunk):
        return pltpu.make_async_remote_copy(
            src_ref=held[stage].at[chunk, :, 1 - bits[stage]],
            dst_ref=landed[stage].at[chunk],
            send_sem=rs_send.at[stage, chunk],
            recv_sem=rs_recv.at[stage, chunk],
            device_id=(ctx, partners[stage]),
            device_id_type=MESH,
        )

    for turn in range(CHUNKS + stages):
        if turn < CHUNKS:
            sides = []
            for h in range(2):
                weights_in[turn][h].wait()
                at = h * side + turn * width
                term = jnp.dot(
                    flat[...], w_buf[:, at : at + width], preferred_element_type=jnp.float32
                )
                sides.append(term.reshape(exp_count, tokens, width))
            both = jnp.concatenate(sides, axis=1).astype(jnp.bfloat16)
            held[0][turn] = both.reshape(exp_count // 2, 2, 2 * tokens, width)
            exchange(0, turn).start()
        for stage in range(stages):
            chunk = turn - 1 - stage
            if chunk < 0 or chunk >= CHUNKS:
                continue
            exchange(stage, chunk).wait_recv()
            mine = held[stage][chunk, :, pl.ds(bits[stage], 1)]
            count = mine.shape[0]
            summed = mine.reshape(count, 2 * tokens, width).astype(jnp.float32)
            summed = summed + landed[stage][chunk].astype(jnp.float32)
            if stage + 1 < stages:
                held[stage + 1][chunk] = summed.astype(jnp.bfloat16).reshape(
                    count // 2, 2, 2 * tokens, width
                )
                exchange(stage + 1, chunk).start()
            else:
                last = summed.reshape(2 * tokens, width)
                for h in range(2):
                    at = h * side + chunk * width
                    out_ref[:, at : at + width] = last[h * tokens : (h + 1) * tokens, :]
    for d in range(ctx_count - 1):
        sends[d].wait_send()
        forwards[d].wait_send()
    for stage in range(stages):
        for chunk in range(CHUNKS):
            exchange(stage, chunk).wait_send()


def attention_call(ctx_count, exp_count, q_rows, latent_t, mask, value_up, output_weight):
    heads, latent_width, vhead = value_up.shape
    rows = q_rows.shape[0] // heads
    key_width, key_rows = latent_t.shape
    model = output_weight.shape[1]
    tokens = rows // exp_count
    stages = exp_count.bit_length() - 1
    width = model // 2 // CHUNKS
    vmem = pl.BlockSpec(memory_space=pltpu.VMEM)
    scratch = [
        pltpu.VMEM((ctx_count, key_width, key_rows), jnp.bfloat16),
        pltpu.VMEM((rows, heads * vhead), jnp.bfloat16),
        pltpu.VMEM(output_weight.shape, jnp.bfloat16),
    ]
    for stage in range(stages):
        blocks = exp_count >> (stage + 1)
        scratch.append(pltpu.VMEM((CHUNKS, blocks, 2, 2 * tokens, width), jnp.bfloat16))
    for stage in range(stages):
        blocks = exp_count >> (stage + 1)
        scratch.append(pltpu.VMEM((CHUNKS, blocks, 2 * tokens, width), jnp.bfloat16))
    dma = pltpu.SemaphoreType.DMA
    scratch += [
        dma((CHUNKS, 2)),
        dma((ctx_count - 1,)),
        dma((ctx_count - 1,)),
        dma((ctx_count - 1,)),
        dma((ctx_count - 1,)),
        dma((stages, CHUNKS)),
        dma((stages, CHUNKS)),
    ]
    return pl.pallas_call(
        functools.partial(attention_kernel, ctx_count, exp_count),
        out_shape=jax.ShapeDtypeStruct((tokens, model), jnp.float32),
        in_specs=[vmem, vmem, vmem, vmem, pl.BlockSpec(memory_space=pl.ANY)],
        out_specs=vmem,
        scratch_shapes=scratch,
        compiler_params=pltpu.CompilerParams(
            collective_id=0, has_side_effects=True, vmem_limit_bytes=48 << 20
        ),
    )(q_rows, latent_t, mask, value_up, output_weight)


def expert_kernel(
    ctx_count,
    exp_count,
    buf_ref,
    gate_hbm,
    up_hbm,
    down_hbm,
    out_ref,
    gate_w,
    up_w,
    down_w,
    recv,
    rows_in,
    ret_in,
    out_buf,
    w_sem,
    d_send,
    d_recv,
    f_send,
    f_recv,
    r_send,
    r_recv,
    b_send,
    b_recv,
):
    ctx = lax.axis_index("ctx")
    exp = lax.axis_index("exp")
    width = buf_ref.shape[2]
    block = buf_ref.shape[1]
    slots = exp_count * block // PIECES
    weights_in = []
    for which, (source, target) in enumerate(((gate_hbm, gate_w), (up_hbm, up_w))):
        for piece in range(PIECES):
            span = pl.ds(piece * width, width)
            weights_in.append(
                pltpu.make_async_copy(
                    source.at[0, span], target.at[span], w_sem.at[which, piece]
                )
            )
    for piece in range(PIECES):
        span = pl.ds(piece * width, width)
        weights_in.append(
            pltpu.make_async_copy(
                down_hbm.at[0, :, span], down_w.at[:, span], w_sem.at[2, piece]
            )
        )
    pending = [w for piece in range(PIECES) for w in (weights_in[piece], weights_in[PIECES + piece])]
    pending = pending + weights_in[2 * PIECES :]

    def fetch(count):
        for copy in pending[:count]:
            copy.start()
        del pending[:count]

    fetch(PIECES)
    stages = exp_count.bit_length() - 1
    to = {}
    for k in range(exp_count):
        partner = exp
        for i in range(stages):
            if (k >> i) & 1:
                partner = partner + (1 - 2 * lax.rem(exp // (1 << i), 2)) * (1 << i)
        to[k] = partner
    origin = to
    quarter = exp_count // 4
    near_last = [2, 3, 1, 0]
    rounds = [[8, 12, 4, 0][n] * exp_count // 16 + m for m in range(quarter) for n in range(4)]
    order = [k for k in rounds if k >= quarter]
    back_order = order + [k for k in near_last + list(range(4, quarter)) if k > 0]
    order = [1] + [k for k in rounds if k > 1]
    others = [lax.rem(ctx + d, ctx_count) for d in range(1, ctx_count)]
    senders = [lax.rem(ctx + ctx_count - d, ctx_count) for d in range(1, ctx_count)]
    greet([(ctx, to[k]) for k in order] + [(o, exp) for o in others])

    def dispatch(k):
        return pltpu.make_async_remote_copy(
            src_ref=buf_ref.at[to[k]],
            dst_ref=recv.at[ctx, exp],
            send_sem=d_send.at[k],
            recv_sem=d_recv.at[k],
            device_id=(ctx, to[k]),
            device_id_type=MESH,
        )

    def forward(d, k):
        return pltpu.make_async_remote_copy(
            src_ref=recv.at[ctx, origin[k]],
            dst_ref=recv.at[ctx, origin[k]],
            send_sem=f_send.at[d, k],
            recv_sem=f_recv.at[d, k],
            device_id=(others[d], exp),
            device_id_type=MESH,
        )

    def give_back(d, k):
        return pltpu.make_async_remote_copy(
            src_ref=recv.at[others[d], to[k]],
            dst_ref=ret_in.at[d, to[k]],
            send_sem=r_send.at[d, k],
            recv_sem=r_recv.at[d, k],
            device_id=(others[d], exp),
            device_id_type=MESH,
        )

    def hand_in(k):
        return pltpu.make_async_remote_copy(
            src_ref=out_buf.at[to[k]],
            dst_ref=out_ref.at[exp],
            send_sem=b_send.at[k],
            recv_sem=b_recv.at[k],
            device_id=(ctx, to[k]),
            device_id_type=MESH,
        )

    for k in order:
        dispatch(k).start()
    recv[ctx, exp] = buf_ref[exp]
    for d in range(ctx_count - 1):
        forward(d, 0).start()
    fetch(PIECES // 2)
    for k in order:
        dispatch(k).wait_recv()
        for d in range(ctx_count - 1):
            forward(d, k).start()
        fetch(1)
    fetch(len(pending))

    row = lax.broadcasted_iota(jnp.int32, (exp_count * block, exp_count * block), 0)
    column = lax.broadcasted_iota(jnp.int32, (exp_count * block, exp_count * block), 1)
    split = jnp.where(
        column == lax.rem(row, slots) * PIECES + row // slots, 1.0, 0.0
    ).astype(jnp.bfloat16)
    merge = jnp.where(
        row == lax.rem(column, slots) * PIECES + column // slots, 1.0, 0.0
    ).astype(jnp.bfloat16)

    def spread(which):
        packed = recv[which].reshape(exp_count * block, width)
        apart = jnp.dot(split, packed, preferred_element_type=jnp.float32).astype(jnp.bfloat16)
        at = pl.ds(pl.multiple_of(which * slots, slots), slots)
        for piece in range(PIECES):
            rows_in[piece, at, :] = apart[piece * slots : (piece + 1) * slots, :]

    spread(ctx)
    for d in range(ctx_count - 1):
        for k in [0] + order:
            forward(d, k).wait_recv()
        spread(senders[d])

    gate = None
    up = None
    for piece in range(PIECES):
        weights_in[piece].wait()
        weights_in[PIECES + piece].wait()
        span = slice(piece * width, (piece + 1) * width)
        rows = rows_in[piece]
        gate_part = jnp.dot(rows, gate_w[span, :], preferred_element_type=jnp.float32)
        up_part = jnp.dot(rows, up_w[span, :], preferred_element_type=jnp.float32)
        gate = gate_part if gate is None else gate + gate_part
        up = up_part if up is None else up + up_part
    inner = (gate / (1.0 + jnp.exp(-gate)) * up).astype(jnp.bfloat16)
    for piece in range(PIECES):
        weights_in[2 * PIECES + piece].wait()
        span = slice(piece * width, (piece + 1) * width)
        result = jnp.dot(inner, down_w[:, span], preferred_element_type=jnp.float32)
        rows_in[piece] = result.astype(jnp.bfloat16)

    for k in order:
        dispatch(k).wait_send()
    for d in range(ctx_count - 1):
        for k in range(exp_count):
            forward(d, k).wait_send()

    def gather(which):
        at = pl.ds(pl.multiple_of(which * slots, slots), slots)
        apart = jnp.concatenate([rows_in[piece, at, :] for piece in range(PIECES)], axis=0)
        packed = jnp.dot(merge, apart, preferred_element_type=jnp.float32).astype(jnp.bfloat16)
        recv[which] = packed.reshape(exp_count, block, width)

    for d in range(ctx_count - 1):
        gather(others[d])
        for k in back_order + [0]:
            give_back(d, k).start()
    gather(ctx)
    for k in back_order + [0]:
        total = recv[ctx, to[k]].astype(jnp.float32)
        for d in range(ctx_count - 1):
            give_back(d, k).wait_recv()
            total = total + ret_in[d, to[k]].astype(jnp.float32)
        if k == 0:
            out_ref[exp] = total.astype(jnp.bfloat16)
        else:
            out_buf[to[k]] = total.astype(jnp.bfloat16)
            hand_in(k).start()
    for k in order:
        hand_in(k).wait_recv()
    for k in order:
        hand_in(k).wait_send()
    for d in range(ctx_count - 1):
        for k in range(exp_count):
            give_back(d, k).wait_send()


def expert_call(ctx_count, exp_count, buffer, gate_weight, up_weight, down_weight):
    block, width = buffer.shape[1:]
    model, hidden = gate_weight.shape[1:]
    slots = exp_count * block // PIECES
    vmem = pl.BlockSpec(memory_space=pltpu.VMEM)
    anywhere = pl.BlockSpec(memory_space=pl.ANY)
    dma = pltpu.SemaphoreType.DMA
    return pl.pallas_call(
        functools.partial(expert_kernel, ctx_count, exp_count),
        out_shape=jax.ShapeDtypeStruct(buffer.shape, jnp.bfloat16),
        in_specs=[vmem, anywhere, anywhere, anywhere],
        out_specs=vmem,
        scratch_shapes=[
            pltpu.VMEM((model, hidden), jnp.bfloat16),
            pltpu.VMEM((model, hidden), jnp.bfloat16),
            pltpu.VMEM((hidden, model), jnp.bfloat16),
            pltpu.VMEM((ctx_count, exp_count, block, width), jnp.bfloat16),
            pltpu.VMEM((PIECES, ctx_count * slots, width), jnp.bfloat16),
            pltpu.VMEM((ctx_count - 1, exp_count, block, width), jnp.bfloat16),
            pltpu.VMEM((exp_count, block, width), jnp.bfloat16),
            dma((3, PIECES)),
            dma((exp_count,)),
            dma((exp_count,)),
            dma((ctx_count - 1, exp_count)),
            dma((ctx_count - 1, exp_count)),
            dma((ctx_count - 1, exp_count)),
            dma((ctx_count - 1, exp_count)),
            dma((exp_count,)),
            dma((exp_count,)),
        ],
        compiler_params=pltpu.CompilerParams(
            collective_id=1, has_side_effects=True, vmem_limit_bytes=62 << 20
        ),
    )(buffer, gate_weight, up_weight, down_weight)


def on_device(
    queries,
    prior_codes,
    fresh_codes,
    prior_powers,
    fresh_powers,
    block_mask,
    value_up,
    output_weight,
    residual,
    norm_gain,
    router,
    route_ids,
    gate_weight,
    up_weight,
    down_weight,
):
    ctx_count = lax.axis_size("ctx")
    exp_count = lax.axis_size("exp")
    ctx_index = lax.axis_index("ctx")
    rows_block, head_count, key_width = queries.shape
    prior_blocks = prior_powers.shape[0]
    own_blocks = prior_blocks + 1
    scales = power_two(jnp.concatenate([prior_powers, fresh_powers], axis=0))
    code_rows = jnp.concatenate([prior_codes, fresh_codes], axis=0)
    latent_t = (
        code_rows.T.astype(jnp.float32) * jnp.repeat(scales, rows_block)[None, :]
    ).astype(jnp.bfloat16)
    q_rows = queries.transpose(1, 0, 2).reshape(head_count * rows_block, key_width)

    mask_row = lax.dynamic_index_in_dim(block_mask, ctx_index, 0, keepdims=False)
    prior_mask = mask_row[: prior_blocks * ctx_count].reshape(ctx_count, prior_blocks)
    fresh_mask = mask_row[prior_blocks * ctx_count :].reshape(ctx_count, 1)
    live = jnp.concatenate([prior_mask, fresh_mask], axis=1) > 0
    position = jnp.arange(rows_block)
    is_fresh = jnp.arange(own_blocks)[None, :] == prior_blocks
    is_own = jnp.arange(ctx_count)[:, None] == ctx_index
    diagonal = jnp.logical_and(is_fresh, is_own)
    causal = position[:, None] >= position[None, :]
    later = jnp.logical_and(is_fresh, jnp.arange(ctx_count)[:, None] > ctx_index)
    live = jnp.logical_and(live, jnp.logical_not(later))
    allowed = jnp.logical_and(
        live[:, None, :, None],
        jnp.logical_or(jnp.logical_not(diagonal)[:, None, :, None], causal[None, :, None, :]),
    )
    mask = allowed.reshape(ctx_count, rows_block, own_blocks * rows_block).astype(jnp.float32)

    attention = attention_call(
        ctx_count, exp_count, q_rows, latent_t, mask, value_up, output_weight
    )
    hidden = (residual.astype(jnp.float32) + attention).astype(jnp.bfloat16)
    hidden_wide = hidden.astype(jnp.float32)
    normed = (
        hidden_wide
        * lax.rsqrt(jnp.mean(hidden_wide * hidden_wide, axis=1, keepdims=True) + 1e-06)
        * norm_gain.astype(jnp.float32)
    ).astype(jnp.bfloat16)
    expert_count = router.shape[1]
    token_count, route_count = route_ids.shape
    model_width = normed.shape[1]
    capacity = token_count * route_count * 2 // expert_count
    affinity = jax.nn.sigmoid(jnp.dot(normed, router, preferred_element_type=jnp.float32))
    route_hits = route_ids[:, :, None] == jnp.arange(expert_count)[None, None, :]
    chosen = jnp.sum(jnp.where(route_hits, affinity[:, None, :], 0.0), axis=2)
    gate_values = 2.5 * chosen / jnp.sum(chosen, axis=1, keepdims=True)
    flat_hits = route_hits.reshape(token_count * route_count, expert_count).astype(jnp.int32)
    before = jnp.cumsum(flat_hits, axis=0) - flat_hits
    slot_index = jnp.sum(before * flat_hits, axis=1)
    target = route_ids.reshape(-1) * capacity + slot_index
    placing = (target[None, :] == jnp.arange(expert_count * capacity)[:, None]).astype(jnp.bfloat16)
    to_token = jnp.sum(placing.reshape(-1, token_count, route_count), axis=2)
    buffer = jnp.dot(to_token, normed, preferred_element_type=jnp.float32).astype(jnp.bfloat16)
    summed = expert_call(
        ctx_count,
        exp_count,
        buffer.reshape(expert_count, capacity * PIECES, model_width // PIECES),
        gate_weight,
        up_weight,
        down_weight,
    ).reshape(expert_count * capacity, model_width)
    gathered_back = jnp.dot(
        jnp.transpose(placing), summed, preferred_element_type=jnp.float32
    ).reshape(token_count, route_count, model_width)
    expert_mix = jnp.sum(gate_values[:, :, None] * gathered_back, axis=1)
    return (hidden_wide + expert_mix).astype(jnp.bfloat16)


def solution(mesh):
    in_specs = (
        P("ctx", "exp", None),
        P("ctx", None),
        P("ctx", None),
        P("ctx"),
        P("ctx"),
        P(),
        P("exp", None, None),
        P("exp", None),
        P(("ctx", "exp"), None),
        P(),
        P(),
        P(("ctx", "exp"), None),
        P("exp", None, "ctx"),
        P("exp", None, "ctx"),
        P("exp", "ctx", None),
    )
    out_specs = P(("ctx", "exp"), None)
    return jax.shard_map(
        on_device, mesh=mesh, in_specs=in_specs, out_specs=out_specs, check_vma=False
    )
```

```python
import functools

import jax
import jax.numpy as jnp
from jax import lax
from jax.experimental import pallas as pl
from jax.experimental.pallas import tpu as pltpu
from jax.sharding import PartitionSpec as P

ROPE = 64
NOPE = 128
MESH = pl.DeviceIdType.MESH
CHUNKS = 7
SWAPPED = (1, 4)
PIECES = 8


def power_two(powers):
    return jnp.where(powers < 0, 0.5, jnp.where(powers > 0, 2.0, 1.0)).astype(jnp.float32)


def greet(peers):
    barrier = pltpu.get_barrier_semaphore()
    for peer in peers:
        pl.semaphore_signal(barrier, inc=1, device_id=peer, device_id_type=MESH)
    pl.semaphore_wait(barrier, len(peers))


def attention_kernel(
    ctx_count,
    exp_count,
    q_ref,
    lat_ref,
    mask_ref,
    up_ref,
    w_hbm,
    out_ref,
    keys,
    flat,
    w_buf,
    *rest,
):
    stages = exp_count.bit_length() - 1
    held = rest[:stages]
    landed = rest[stages : 2 * stages]
    w_sem, lat_send, lat_recv, fwd_send, fwd_recv, rs_send, rs_recv = rest[2 * stages :]
    ctx = lax.axis_index("ctx")
    exp = lax.axis_index("exp")
    heads, latent_width, vhead = up_ref.shape
    rows = q_ref.shape[0] // heads
    key_width, key_rows = lat_ref.shape
    half = key_width // 2
    model = out_ref.shape[1]
    side = model // 2
    width = side // CHUNKS
    bits = [lax.rem(exp // (1 << i), 2) for i in range(stages)]
    partners = [exp + (1 - 2 * bits[i]) * (1 << i) for i in range(stages)]

    others = [lax.rem(ctx + d, ctx_count) for d in range(1, ctx_count)]
    senders = [lax.rem(ctx + ctx_count - d, ctx_count) for d in range(1, ctx_count)]
    greet([(o, exp) for o in others] + [(ctx, p) for p in partners])

    part = pl.ds(pl.multiple_of(bits[0] * half, half), half)
    sends = []
    for d, other in enumerate(others):
        copy = pltpu.make_async_remote_copy(
            src_ref=lat_ref.at[part],
            dst_ref=keys.at[ctx, part],
            send_sem=lat_send.at[d],
            recv_sem=lat_recv.at[d],
            device_id=(other, exp),
            device_id_type=MESH,
        )
        copy.start()
        sends.append(copy)
    weights_in = []
    for chunk in range(CHUNKS):
        pair = []
        for h in range(2):
            columns = pl.ds(h * side + chunk * width, width)
            copy = pltpu.make_async_copy(
                w_hbm.at[:, columns], w_buf.at[:, columns], w_sem.at[chunk, h]
            )
            copy.start()
            pair.append(copy)
        weights_in.append(pair)


    factor = 1.0 / (NOPE + ROPE) ** 0.5

    def attend(h, key_block, live):
        q_head = q_ref[h * rows : (h + 1) * rows, :]
        raw = jnp.dot(q_head, key_block[...], preferred_element_type=jnp.float32) * factor
        raw = jnp.where(live, raw, -1e30)
        top = jnp.max(raw, axis=1, keepdims=True)
        weights = jnp.where(live, jnp.exp(raw - top), 0.0)
        total = jnp.sum(weights, axis=1, keepdims=True)
        mixture = lax.dot_general(
            weights.astype(jnp.bfloat16),
            key_block[:latent_width, :],
            (((1,), (1,)), ((), ())),
            preferred_element_type=jnp.float32,
        )
        return top, total, mixture

    live = mask_ref[ctx] > 0
    states = [attend(h, lat_ref, live) for h in range(heads)]
    forwards = []
    for d, sender in enumerate(senders):
        sends[d].wait_recv()
        copy = pltpu.make_async_remote_copy(
            src_ref=keys.at[sender, part],
            dst_ref=keys.at[sender, part],
            send_sem=fwd_send.at[d],
            recv_sem=fwd_recv.at[d],
            device_id=(ctx, partners[0]),
            device_id_type=MESH,
        )
        copy.start()
        forwards.append(copy)
    for d, sender in enumerate(senders):
        forwards[d].wait_recv()
        live = mask_ref[sender] > 0
        for h in range(heads):
            top, total, mixture = states[h]
            new_top, new_total, new_mixture = attend(h, keys.at[sender], live)
            both_top = jnp.maximum(top, new_top)
            shrink = jnp.exp(top - both_top)
            new_shrink = jnp.exp(new_top - both_top)
            states[h] = (
                both_top,
                total * shrink + new_total * new_shrink,
                mixture * shrink + new_mixture * new_shrink,
            )
    for h in range(heads):
        top, total, mixture = states[h]
        attended = (mixture / total).astype(jnp.bfloat16)
        head_out = jnp.dot(attended, up_ref[h], preferred_element_type=jnp.float32)
        flat[:, h * vhead : (h + 1) * vhead] = head_out.astype(jnp.bfloat16)

    tokens = rows // exp_count

    def axis_of(stage, chunk):
        if chunk in SWAPPED and stage in (1, 2) and stages > 2:
            return 3 - stage
        return stage

    def exchange(stage, chunk):
        bit = axis_of(stage, chunk)
        return pltpu.make_async_remote_copy(
            src_ref=held[stage].at[chunk, :, 1 - bits[bit]],
            dst_ref=landed[stage].at[chunk],
            send_sem=rs_send.at[stage, chunk],
            recv_sem=rs_recv.at[stage, chunk],
            device_id=(ctx, partners[bit]),
            device_id_type=MESH,
        )

    for turn in range(CHUNKS + stages):
        if turn < CHUNKS:
            sides = []
            for h in range(2):
                weights_in[turn][h].wait()
                at = h * side + turn * width
                term = jnp.dot(
                    flat[...], w_buf[:, at : at + width], preferred_element_type=jnp.float32
                )
                sides.append(term.reshape(exp_count, tokens, width))
            both = jnp.concatenate(sides, axis=1).astype(jnp.bfloat16)
            held[0][turn] = both.reshape(exp_count // 2, 2, 2 * tokens, width)
            exchange(0, turn).start()
        for stage in range(stages):
            chunk = turn - 1 - stage
            if chunk < 0 or chunk >= CHUNKS:
                continue
            exchange(stage, chunk).wait_recv()
            mine = held[stage][chunk, :, pl.ds(bits[axis_of(stage, chunk)], 1)]
            count = mine.shape[0]
            summed = mine.reshape(count, 2 * tokens, width).astype(jnp.float32)
            summed = summed + landed[stage][chunk].astype(jnp.float32)
            if stage == 0 and axis_of(1, chunk) != 1:
                summed = jnp.stack(
                    [
                        summed[b * 4 + second * 2 + first]
                        for b in range(count // 4)
                        for first in range(2)
                        for second in range(2)
                    ]
                )
            if stage + 1 < stages:
                held[stage + 1][chunk] = summed.astype(jnp.bfloat16).reshape(
                    count // 2, 2, 2 * tokens, width
                )
                exchange(stage + 1, chunk).start()
            else:
                last = summed.reshape(2 * tokens, width)
                for h in range(2):
                    at = h * side + chunk * width
                    out_ref[:, at : at + width] = last[h * tokens : (h + 1) * tokens, :]
    for d in range(ctx_count - 1):
        sends[d].wait_send()
        forwards[d].wait_send()
    for stage in range(stages):
        for chunk in range(CHUNKS):
            exchange(stage, chunk).wait_send()


def attention_call(ctx_count, exp_count, q_rows, latent_t, mask, value_up, output_weight):
    heads, latent_width, vhead = value_up.shape
    rows = q_rows.shape[0] // heads
    key_width, key_rows = latent_t.shape
    model = output_weight.shape[1]
    tokens = rows // exp_count
    stages = exp_count.bit_length() - 1
    width = model // 2 // CHUNKS
    vmem = pl.BlockSpec(memory_space=pltpu.VMEM)
    scratch = [
        pltpu.VMEM((ctx_count, key_width, key_rows), jnp.bfloat16),
        pltpu.VMEM((rows, heads * vhead), jnp.bfloat16),
        pltpu.VMEM(output_weight.shape, jnp.bfloat16),
    ]
    for stage in range(stages):
        blocks = exp_count >> (stage + 1)
        scratch.append(pltpu.VMEM((CHUNKS, blocks, 2, 2 * tokens, width), jnp.bfloat16))
    for stage in range(stages):
        blocks = exp_count >> (stage + 1)
        scratch.append(pltpu.VMEM((CHUNKS, blocks, 2 * tokens, width), jnp.bfloat16))
    dma = pltpu.SemaphoreType.DMA
    scratch += [
        dma((CHUNKS, 2)),
        dma((ctx_count - 1,)),
        dma((ctx_count - 1,)),
        dma((ctx_count - 1,)),
        dma((ctx_count - 1,)),
        dma((stages, CHUNKS)),
        dma((stages, CHUNKS)),
    ]
    return pl.pallas_call(
        functools.partial(attention_kernel, ctx_count, exp_count),
        out_shape=jax.ShapeDtypeStruct((tokens, model), jnp.float32),
        in_specs=[vmem, vmem, vmem, vmem, pl.BlockSpec(memory_space=pl.ANY)],
        out_specs=vmem,
        scratch_shapes=scratch,
        compiler_params=pltpu.CompilerParams(
            collective_id=0, has_side_effects=True, vmem_limit_bytes=48 << 20
        ),
    )(q_rows, latent_t, mask, value_up, output_weight)


def expert_kernel(
    ctx_count,
    exp_count,
    pick_ref,
    stack_ref,
    gate_hbm,
    up_hbm,
    down_hbm,
    out_ref,
    buf_ref,
    back,
    gate_w,
    up_w,
    down_w,
    recv,
    rows_in,
    ret_in,
    out_buf,
    w_sem,
    d_send,
    d_recv,
    f_send,
    f_recv,
    r_send,
    r_recv,
    b_send,
    b_recv,
):
    ctx = lax.axis_index("ctx")
    exp = lax.axis_index("exp")
    width = buf_ref.shape[2]
    block = buf_ref.shape[1]
    slots = exp_count * block // PIECES
    weights_in = []
    for which, (source, target) in enumerate(((gate_hbm, gate_w), (up_hbm, up_w))):
        for piece in range(PIECES):
            span = pl.ds(piece * width, width)
            weights_in.append(
                pltpu.make_async_copy(
                    source.at[0, span], target.at[span], w_sem.at[which, piece]
                )
            )
    for piece in range(PIECES):
        span = pl.ds(piece * width, width)
        weights_in.append(
            pltpu.make_async_copy(
                down_hbm.at[0, :, span], down_w.at[:, span], w_sem.at[2, piece]
            )
        )
    pending = [w for piece in range(PIECES) for w in (weights_in[piece], weights_in[PIECES + piece])]
    pending = pending + weights_in[2 * PIECES :]

    def fetch(count):
        for copy in pending[:count]:
            copy.start()
        del pending[:count]

    fetch(PIECES)
    routes = pick_ref.shape[0] // stack_ref.shape[0]
    placed = lax.dot_general(
        pick_ref[...],
        jnp.concatenate([stack_ref[...]] * routes, axis=0),
        (((0,), (0,)), ((), ())),
        preferred_element_type=jnp.float32,
    )
    buf_ref[...] = placed.astype(jnp.bfloat16).reshape(exp_count, block, width)
    stages = exp_count.bit_length() - 1
    to = {}
    for k in range(exp_count):
        partner = exp
        for i in range(stages):
            if (k >> i) & 1:
                partner = partner + (1 - 2 * lax.rem(exp // (1 << i), 2)) * (1 << i)
        to[k] = partner
    origin = to
    quarter = exp_count // 4
    near_last = [2, 3, 1, 0]
    rounds = [[8, 12, 4, 0][n] * exp_count // 16 + m for m in range(quarter) for n in range(4)]
    order = [k for k in rounds if k >= quarter]
    back_order = order + [k for k in near_last + list(range(4, quarter)) if k > 0]
    order = [1] + [k for k in rounds if k > 1]
    others = [lax.rem(ctx + d, ctx_count) for d in range(1, ctx_count)]
    senders = [lax.rem(ctx + ctx_count - d, ctx_count) for d in range(1, ctx_count)]
    greet([(ctx, to[k]) for k in order] + [(o, exp) for o in others])

    def dispatch(k):
        return pltpu.make_async_remote_copy(
            src_ref=buf_ref.at[to[k]],
            dst_ref=recv.at[ctx, exp],
            send_sem=d_send.at[k],
            recv_sem=d_recv.at[k],
            device_id=(ctx, to[k]),
            device_id_type=MESH,
        )

    def forward(d, k):
        return pltpu.make_async_remote_copy(
            src_ref=recv.at[ctx, origin[k]],
            dst_ref=recv.at[ctx, origin[k]],
            send_sem=f_send.at[d, k],
            recv_sem=f_recv.at[d, k],
            device_id=(others[d], exp),
            device_id_type=MESH,
        )

    def give_back(d, k):
        return pltpu.make_async_remote_copy(
            src_ref=recv.at[others[d], to[k]],
            dst_ref=ret_in.at[d, to[k]],
            send_sem=r_send.at[d, k],
            recv_sem=r_recv.at[d, k],
            device_id=(others[d], exp),
            device_id_type=MESH,
        )

    def hand_in(k):
        return pltpu.make_async_remote_copy(
            src_ref=out_buf.at[to[k]],
            dst_ref=back.at[exp],
            send_sem=b_send.at[k],
            recv_sem=b_recv.at[k],
            device_id=(ctx, to[k]),
            device_id_type=MESH,
        )

    for k in order:
        dispatch(k).start()
    recv[ctx, exp] = buf_ref[exp]
    for d in range(ctx_count - 1):
        forward(d, 0).start()
    fetch(PIECES // 2)
    row = lax.broadcasted_iota(jnp.int32, (exp_count * block, exp_count * block), 0)
    column = lax.broadcasted_iota(jnp.int32, (exp_count * block, exp_count * block), 1)
    span_bits = slots.bit_length() - 1
    split = jnp.where(
        column == (row & (slots - 1)) * PIECES + (row >> span_bits), 1.0, 0.0
    ).astype(jnp.bfloat16)
    merge = jnp.where(
        row == (column & (slots - 1)) * PIECES + (column >> span_bits), 1.0, 0.0
    ).astype(jnp.bfloat16)
    for k in order:
        dispatch(k).wait_recv()
        for d in range(ctx_count - 1):
            forward(d, k).start()
        fetch(1)
    fetch(len(pending))

    def spread(which):
        packed = recv[which].reshape(exp_count * block, width)
        apart = jnp.dot(split, packed, preferred_element_type=jnp.float32).astype(jnp.bfloat16)
        at = pl.ds(pl.multiple_of(which * slots, slots), slots)
        for piece in range(PIECES):
            rows_in[piece, at, :] = apart[piece * slots : (piece + 1) * slots, :]

    spread(ctx)
    for d in range(ctx_count - 1):
        for k in [0] + order:
            forward(d, k).wait_recv()
        spread(senders[d])

    gate = None
    up = None
    for piece in range(PIECES):
        weights_in[piece].wait()
        weights_in[PIECES + piece].wait()
        span = slice(piece * width, (piece + 1) * width)
        rows = rows_in[piece]
        gate_part = jnp.dot(rows, gate_w[span, :], preferred_element_type=jnp.float32)
        up_part = jnp.dot(rows, up_w[span, :], preferred_element_type=jnp.float32)
        gate = gate_part if gate is None else gate + gate_part
        up = up_part if up is None else up + up_part
    inner = (gate / (1.0 + jnp.exp(-gate)) * up).astype(jnp.bfloat16)
    for piece in range(PIECES):
        weights_in[2 * PIECES + piece].wait()
        span = slice(piece * width, (piece + 1) * width)
        result = jnp.dot(inner, down_w[:, span], preferred_element_type=jnp.float32)
        rows_in[piece] = result.astype(jnp.bfloat16)

    for k in order:
        dispatch(k).wait_send()
    for d in range(ctx_count - 1):
        for k in range(exp_count):
            forward(d, k).wait_send()

    def gather(which):
        at = pl.ds(pl.multiple_of(which * slots, slots), slots)
        apart = jnp.concatenate([rows_in[piece, at, :] for piece in range(PIECES)], axis=0)
        packed = jnp.dot(merge, apart, preferred_element_type=jnp.float32).astype(jnp.bfloat16)
        recv[which] = packed.reshape(exp_count, block, width)

    for d in range(ctx_count - 1):
        gather(others[d])
        for k in back_order + [0]:
            give_back(d, k).start()
    gather(ctx)
    for k in back_order + [0]:
        total = recv[ctx, to[k]].astype(jnp.float32)
        for d in range(ctx_count - 1):
            give_back(d, k).wait_recv()
            total = total + ret_in[d, to[k]].astype(jnp.float32)
        if k == 0:
            back[exp] = total.astype(jnp.bfloat16)
        else:
            out_buf[to[k]] = total.astype(jnp.bfloat16)
            hand_in(k).start()
    for k in order:
        hand_in(k).wait_recv()
    packed = back[...].reshape(exp_count * block, width)
    taken = jnp.dot(pick_ref[...], packed, preferred_element_type=jnp.float32)
    out_ref[...] = taken.astype(jnp.bfloat16)
    for k in order:
        hand_in(k).wait_send()
    for d in range(ctx_count - 1):
        for k in range(exp_count):
            give_back(d, k).wait_send()


def expert_call(ctx_count, exp_count, pick, stack, gate_weight, up_weight, down_weight):
    block = pick.shape[1] // exp_count
    width = stack.shape[1]
    model, hidden = gate_weight.shape[1:]
    slots = exp_count * block // PIECES
    vmem = pl.BlockSpec(memory_space=pltpu.VMEM)
    anywhere = pl.BlockSpec(memory_space=pl.ANY)
    dma = pltpu.SemaphoreType.DMA
    return pl.pallas_call(
        functools.partial(expert_kernel, ctx_count, exp_count),
        out_shape=jax.ShapeDtypeStruct((pick.shape[0], width), jnp.bfloat16),
        in_specs=[vmem, vmem, anywhere, anywhere, anywhere],
        out_specs=vmem,
        scratch_shapes=[
            pltpu.VMEM((exp_count, block, width), jnp.bfloat16),
            pltpu.VMEM((exp_count, block, width), jnp.bfloat16),
            pltpu.VMEM((model, hidden), jnp.bfloat16),
            pltpu.VMEM((model, hidden), jnp.bfloat16),
            pltpu.VMEM((hidden, model), jnp.bfloat16),
            pltpu.VMEM((ctx_count, exp_count, block, width), jnp.bfloat16),
            pltpu.VMEM((PIECES, ctx_count * slots, width), jnp.bfloat16),
            pltpu.VMEM((ctx_count - 1, exp_count, block, width), jnp.bfloat16),
            pltpu.VMEM((exp_count, block, width), jnp.bfloat16),
            dma((3, PIECES)),
            dma((exp_count,)),
            dma((exp_count,)),
            dma((ctx_count - 1, exp_count)),
            dma((ctx_count - 1, exp_count)),
            dma((ctx_count - 1, exp_count)),
            dma((ctx_count - 1, exp_count)),
            dma((exp_count,)),
            dma((exp_count,)),
        ],
        compiler_params=pltpu.CompilerParams(
            collective_id=1, has_side_effects=True, vmem_limit_bytes=62 << 20
        ),
    )(pick, stack, gate_weight, up_weight, down_weight)


def on_device(
    queries,
    prior_codes,
    fresh_codes,
    prior_powers,
    fresh_powers,
    block_mask,
    value_up,
    output_weight,
    residual,
    norm_gain,
    router,
    route_ids,
    gate_weight,
    up_weight,
    down_weight,
):
    ctx_count = lax.axis_size("ctx")
    exp_count = lax.axis_size("exp")
    ctx_index = lax.axis_index("ctx")
    rows_block, head_count, key_width = queries.shape
    prior_blocks = prior_powers.shape[0]
    own_blocks = prior_blocks + 1
    scales = power_two(jnp.concatenate([prior_powers, fresh_powers], axis=0))
    code_rows = jnp.concatenate([prior_codes, fresh_codes], axis=0)
    latent_t = (
        code_rows.T.astype(jnp.float32) * jnp.repeat(scales, rows_block)[None, :]
    ).astype(jnp.bfloat16)
    q_rows = queries.transpose(1, 0, 2).reshape(head_count * rows_block, key_width)

    mask_row = lax.dynamic_index_in_dim(block_mask, ctx_index, 0, keepdims=False)
    prior_mask = mask_row[: prior_blocks * ctx_count].reshape(ctx_count, prior_blocks)
    fresh_mask = mask_row[prior_blocks * ctx_count :].reshape(ctx_count, 1)
    live = jnp.concatenate([prior_mask, fresh_mask], axis=1) > 0
    position = jnp.arange(rows_block)
    is_fresh = jnp.arange(own_blocks)[None, :] == prior_blocks
    is_own = jnp.arange(ctx_count)[:, None] == ctx_index
    diagonal = jnp.logical_and(is_fresh, is_own)
    causal = position[:, None] >= position[None, :]
    later = jnp.logical_and(is_fresh, jnp.arange(ctx_count)[:, None] > ctx_index)
    live = jnp.logical_and(live, jnp.logical_not(later))
    allowed = jnp.logical_and(
        live[:, None, :, None],
        jnp.logical_or(jnp.logical_not(diagonal)[:, None, :, None], causal[None, :, None, :]),
    )
    mask = allowed.reshape(ctx_count, rows_block, own_blocks * rows_block).astype(jnp.float32)

    attention = attention_call(
        ctx_count, exp_count, q_rows, latent_t, mask, value_up, output_weight
    )
    hidden = (residual.astype(jnp.float32) + attention).astype(jnp.bfloat16)
    hidden_wide = hidden.astype(jnp.float32)
    normed = (
        hidden_wide
        * lax.rsqrt(jnp.mean(hidden_wide * hidden_wide, axis=1, keepdims=True) + 1e-06)
        * norm_gain.astype(jnp.float32)
    ).astype(jnp.bfloat16)
    expert_count = router.shape[1]
    token_count, route_count = route_ids.shape
    model_width = normed.shape[1]
    capacity = token_count * route_count * 2 // expert_count
    affinity = jax.nn.sigmoid(jnp.dot(normed, router, preferred_element_type=jnp.float32))
    route_hits = route_ids[:, :, None] == jnp.arange(expert_count)[None, None, :]
    chosen = jnp.sum(jnp.where(route_hits, affinity[:, None, :], 0.0), axis=2)
    gate_values = 2.5 * chosen / jnp.sum(chosen, axis=1, keepdims=True)
    flat_hits = route_hits.reshape(token_count * route_count, expert_count).astype(jnp.int32)
    before = jnp.cumsum(flat_hits, axis=0) - flat_hits
    slot_index = jnp.sum(before * flat_hits, axis=1)
    target = (route_ids.reshape(-1) * capacity + slot_index).reshape(token_count, route_count)
    place = target.T[:, None, :] * PIECES + jnp.arange(PIECES)[None, :, None]
    pick = (
        place.reshape(-1)[:, None] == jnp.arange(expert_count * capacity * PIECES)[None, :]
    ).astype(jnp.bfloat16)
    width = model_width // PIECES
    stack = normed.reshape(token_count, PIECES, width).transpose(1, 0, 2)
    taken = expert_call(
        ctx_count,
        exp_count,
        pick,
        stack.reshape(PIECES * token_count, width),
        gate_weight,
        up_weight,
        down_weight,
    ).reshape(route_count, PIECES, token_count, width)
    gates = gate_values.T[:, None, :, None]
    expert_mix = jnp.sum(gates * taken.astype(jnp.float32), axis=0)
    expert_mix = expert_mix.transpose(1, 0, 2).reshape(token_count, model_width)
    return (hidden_wide + expert_mix).astype(jnp.bfloat16)


def solution(mesh):
    in_specs = (
        P("ctx", "exp", None),
        P("ctx", None),
        P("ctx", None),
        P("ctx"),
        P("ctx"),
        P(),
        P("exp", None, None),
        P("exp", None),
        P(("ctx", "exp"), None),
        P(),
        P(),
        P(("ctx", "exp"), None),
        P("exp", None, "ctx"),
        P("exp", None, "ctx"),
        P("exp", "ctx", None),
    )
    out_specs = P(("ctx", "exp"), None)
    return jax.shard_map(
        on_device, mesh=mesh, in_specs=in_specs, out_specs=out_specs, check_vma=False
    )
```

```python
import functools

import jax
import jax.numpy as jnp
from jax import lax
from jax.experimental import pallas as pl
from jax.experimental.pallas import tpu as pltpu
from jax.sharding import PartitionSpec as P

ROPE = 64
NOPE = 128
MESH = pl.DeviceIdType.MESH
CHUNKS = 4
PIECES = 8


def power_two(powers):
    return jnp.where(powers < 0, 0.5, jnp.where(powers > 0, 2.0, 1.0)).astype(jnp.float32)


def greet(peers):
    barrier = pltpu.get_barrier_semaphore()
    for peer in peers:
        pl.semaphore_signal(barrier, inc=1, device_id=peer, device_id_type=MESH)
    pl.semaphore_wait(barrier, len(peers))


def attention_kernel(
    ctx_count,
    exp_count,
    q_ref,
    lat_ref,
    mask_ref,
    up_ref,
    w_hbm,
    out_ref,
    keys,
    flat,
    w_buf,
    *rest,
):
    stages = exp_count.bit_length() - 1
    held = rest[:stages]
    landed = rest[stages : 2 * stages]
    w_sem, lat_send, lat_recv, fwd_send, fwd_recv, rs_send, rs_recv = rest[2 * stages :]
    ctx = lax.axis_index("ctx")
    exp = lax.axis_index("exp")
    heads, latent_width, vhead = up_ref.shape
    rows = q_ref.shape[0] // heads
    key_width, key_rows = lat_ref.shape
    half = key_width // 2
    model = out_ref.shape[1]
    side = model // 2
    width = side // CHUNKS
    bits = [lax.rem(exp // (1 << i), 2) for i in range(stages)]
    partners = [exp + (1 - 2 * bits[i]) * (1 << i) for i in range(stages)]

    others = [lax.rem(ctx + d, ctx_count) for d in range(1, ctx_count)]
    senders = [lax.rem(ctx + ctx_count - d, ctx_count) for d in range(1, ctx_count)]
    greet([(o, exp) for o in others] + [(ctx, p) for p in partners])

    part = pl.ds(pl.multiple_of(bits[0] * half, half), half)
    sends = []
    for d, other in enumerate(others):
        copy = pltpu.make_async_remote_copy(
            src_ref=lat_ref.at[part],
            dst_ref=keys.at[ctx, part],
            send_sem=lat_send.at[d],
            recv_sem=lat_recv.at[d],
            device_id=(other, exp),
            device_id_type=MESH,
        )
        copy.start()
        sends.append(copy)
    weights_in = []
    for chunk in range(CHUNKS):
        pair = []
        for h in range(2):
            columns = pl.ds(h * side + chunk * width, width)
            copy = pltpu.make_async_copy(
                w_hbm.at[:, columns], w_buf.at[:, columns], w_sem.at[chunk, h]
            )
            copy.start()
            pair.append(copy)
        weights_in.append(pair)


    factor = 1.0 / (NOPE + ROPE) ** 0.5

    def attend(h, key_block, live):
        q_head = q_ref[h * rows : (h + 1) * rows, :]
        raw = jnp.dot(q_head, key_block[...], preferred_element_type=jnp.float32) * factor
        raw = jnp.where(live, raw, -1e30)
        top = jnp.max(raw, axis=1, keepdims=True)
        weights = jnp.where(live, jnp.exp(raw - top), 0.0)
        total = jnp.sum(weights, axis=1, keepdims=True)
        mixture = lax.dot_general(
            weights.astype(jnp.bfloat16),
            key_block[:latent_width, :],
            (((1,), (1,)), ((), ())),
            preferred_element_type=jnp.float32,
        )
        return top, total, mixture

    live = mask_ref[ctx] > 0
    states = [attend(h, lat_ref, live) for h in range(heads)]
    forwards = []
    for d, sender in enumerate(senders):
        sends[d].wait_recv()
        copy = pltpu.make_async_remote_copy(
            src_ref=keys.at[sender, part],
            dst_ref=keys.at[sender, part],
            send_sem=fwd_send.at[d],
            recv_sem=fwd_recv.at[d],
            device_id=(ctx, partners[0]),
            device_id_type=MESH,
        )
        copy.start()
        forwards.append(copy)
    for d, sender in enumerate(senders):
        forwards[d].wait_recv()
        live = mask_ref[sender] > 0
        for h in range(heads):
            top, total, mixture = states[h]
            new_top, new_total, new_mixture = attend(h, keys.at[sender], live)
            both_top = jnp.maximum(top, new_top)
            shrink = jnp.exp(top - both_top)
            new_shrink = jnp.exp(new_top - both_top)
            states[h] = (
                both_top,
                total * shrink + new_total * new_shrink,
                mixture * shrink + new_mixture * new_shrink,
            )
    for h in range(heads):
        top, total, mixture = states[h]
        attended = (mixture / total).astype(jnp.bfloat16)
        head_out = jnp.dot(attended, up_ref[h], preferred_element_type=jnp.float32)
        flat[:, h * vhead : (h + 1) * vhead] = head_out.astype(jnp.bfloat16)

    tokens = rows // exp_count

    def exchange(stage, chunk):
        return pltpu.make_async_remote_copy(
            src_ref=held[stage].at[chunk, :, 1 - bits[stage]],
            dst_ref=landed[stage].at[chunk],
            send_sem=rs_send.at[stage, chunk],
            recv_sem=rs_recv.at[stage, chunk],
            device_id=(ctx, partners[stage]),
            device_id_type=MESH,
        )

    for turn in range(CHUNKS + stages):
        if turn < CHUNKS:
            sides = []
            for h in range(2):
                weights_in[turn][h].wait()
                at = h * side + turn * width
                term = jnp.dot(
                    flat[...], w_buf[:, at : at + width], preferred_element_type=jnp.float32
                )
                sides.append(term.reshape(exp_count, tokens, width))
            both = jnp.concatenate(sides, axis=1).astype(jnp.bfloat16)
            held[0][turn] = both.reshape(exp_count // 2, 2, 2 * tokens, width)
            exchange(0, turn).start()
        for stage in range(stages):
            chunk = turn - 1 - stage
            if chunk < 0 or chunk >= CHUNKS:
                continue
            exchange(stage, chunk).wait_recv()
            mine = held[stage][chunk, :, pl.ds(bits[stage], 1)]
            count = mine.shape[0]
            summed = mine.reshape(count, 2 * tokens, width).astype(jnp.float32)
            summed = summed + landed[stage][chunk].astype(jnp.float32)
            if stage + 1 < stages:
                held[stage + 1][chunk] = summed.astype(jnp.bfloat16).reshape(
                    count // 2, 2, 2 * tokens, width
                )
                exchange(stage + 1, chunk).start()
            else:
                last = summed.reshape(2 * tokens, width)
                for h in range(2):
                    at = h * side + chunk * width
                    out_ref[:, at : at + width] = last[h * tokens : (h + 1) * tokens, :]
    for d in range(ctx_count - 1):
        sends[d].wait_send()
        forwards[d].wait_send()
    for stage in range(stages):
        for chunk in range(CHUNKS):
            exchange(stage, chunk).wait_send()


def attention_call(ctx_count, exp_count, q_rows, latent_t, mask, value_up, output_weight):
    heads, latent_width, vhead = value_up.shape
    rows = q_rows.shape[0] // heads
    key_width, key_rows = latent_t.shape
    model = output_weight.shape[1]
    tokens = rows // exp_count
    stages = exp_count.bit_length() - 1
    width = model // 2 // CHUNKS
    vmem = pl.BlockSpec(memory_space=pltpu.VMEM)
    scratch = [
        pltpu.VMEM((ctx_count, key_width, key_rows), jnp.bfloat16),
        pltpu.VMEM((rows, heads * vhead), jnp.bfloat16),
        pltpu.VMEM(output_weight.shape, jnp.bfloat16),
    ]
    for stage in range(stages):
        blocks = exp_count >> (stage + 1)
        scratch.append(pltpu.VMEM((CHUNKS, blocks, 2, 2 * tokens, width), jnp.bfloat16))
    for stage in range(stages):
        blocks = exp_count >> (stage + 1)
        scratch.append(pltpu.VMEM((CHUNKS, blocks, 2 * tokens, width), jnp.bfloat16))
    dma = pltpu.SemaphoreType.DMA
    scratch += [
        dma((CHUNKS, 2)),
        dma((ctx_count - 1,)),
        dma((ctx_count - 1,)),
        dma((ctx_count - 1,)),
        dma((ctx_count - 1,)),
        dma((stages, CHUNKS)),
        dma((stages, CHUNKS)),
    ]
    return pl.pallas_call(
        functools.partial(attention_kernel, ctx_count, exp_count),
        out_shape=jax.ShapeDtypeStruct((tokens, model), jnp.float32),
        in_specs=[vmem, vmem, vmem, vmem, pl.BlockSpec(memory_space=pl.ANY)],
        out_specs=vmem,
        scratch_shapes=scratch,
        compiler_params=pltpu.CompilerParams(
            collective_id=0, has_side_effects=True, vmem_limit_bytes=48 << 20
        ),
    )(q_rows, latent_t, mask, value_up, output_weight)


def expert_kernel(
    ctx_count,
    exp_count,
    pick_ref,
    stack_ref,
    gate_hbm,
    up_hbm,
    down_hbm,
    out_ref,
    buf_ref,
    back,
    gate_w,
    up_w,
    down_w,
    recv,
    rows_in,
    ret_in,
    out_buf,
    w_sem,
    d_send,
    d_recv,
    f_send,
    f_recv,
    r_send,
    r_recv,
    b_send,
    b_recv,
):
    ctx = lax.axis_index("ctx")
    exp = lax.axis_index("exp")
    width = buf_ref.shape[2]
    block = buf_ref.shape[1]
    slots = exp_count * block // PIECES
    weights_in = []
    for which, (source, target) in enumerate(((gate_hbm, gate_w), (up_hbm, up_w))):
        for piece in range(PIECES):
            span = pl.ds(piece * width, width)
            weights_in.append(
                pltpu.make_async_copy(
                    source.at[0, span], target.at[span], w_sem.at[which, piece]
                )
            )
    for piece in range(PIECES):
        span = pl.ds(piece * width, width)
        weights_in.append(
            pltpu.make_async_copy(
                down_hbm.at[0, :, span], down_w.at[:, span], w_sem.at[2, piece]
            )
        )
    pending = [w for piece in range(PIECES) for w in (weights_in[piece], weights_in[PIECES + piece])]
    pending = pending + weights_in[2 * PIECES :]

    def fetch(count):
        for copy in pending[:count]:
            copy.start()
        del pending[:count]

    fetch(PIECES)
    routes = pick_ref.shape[0] // stack_ref.shape[0]
    placed = lax.dot_general(
        pick_ref[...],
        jnp.concatenate([stack_ref[...]] * routes, axis=0),
        (((0,), (0,)), ((), ())),
        preferred_element_type=jnp.float32,
    )
    buf_ref[...] = placed.astype(jnp.bfloat16).reshape(exp_count, block, width)
    stages = exp_count.bit_length() - 1
    to = {}
    for k in range(exp_count):
        partner = exp
        for i in range(stages):
            if (k >> i) & 1:
                partner = partner + (1 - 2 * lax.rem(exp // (1 << i), 2)) * (1 << i)
        to[k] = partner
    quarter = exp_count // 4
    tops = [2 * quarter, 3 * quarter, quarter, 0]
    pairs = [top + low for low in range(0, quarter, 2) for top in tops]
    back_pairs = [p for p in pairs if p >= quarter] + [p for p in reversed(range(0, quarter, 2))]
    pairs = [0] + [p for p in pairs if p > 0]
    order = [k for p in pairs for k in (p, p + 1) if k > 0]
    spans = {p: pl.ds(to[p] // 2 * 2, 2) for p in pairs}
    others = [lax.rem(ctx + d, ctx_count) for d in range(1, ctx_count)]
    senders = [lax.rem(ctx + ctx_count - d, ctx_count) for d in range(1, ctx_count)]
    greet([(ctx, to[k]) for k in order] + [(o, exp) for o in others])

    def dispatch(k):
        return pltpu.make_async_remote_copy(
            src_ref=buf_ref.at[to[k]],
            dst_ref=recv.at[ctx, exp],
            send_sem=d_send.at[k],
            recv_sem=d_recv.at[k],
            device_id=(ctx, to[k]),
            device_id_type=MESH,
        )

    def forward(d, p):
        return pltpu.make_async_remote_copy(
            src_ref=recv.at[ctx, spans[p]],
            dst_ref=recv.at[ctx, spans[p]],
            send_sem=f_send.at[d, p],
            recv_sem=f_recv.at[d, p],
            device_id=(others[d], exp),
            device_id_type=MESH,
        )

    def give_back(d, p):
        return pltpu.make_async_remote_copy(
            src_ref=recv.at[others[d], spans[p]],
            dst_ref=ret_in.at[d, spans[p]],
            send_sem=r_send.at[d, p],
            recv_sem=r_recv.at[d, p],
            device_id=(others[d], exp),
            device_id_type=MESH,
        )

    def hand_in(k):
        return pltpu.make_async_remote_copy(
            src_ref=out_buf.at[to[k]],
            dst_ref=back.at[exp],
            send_sem=b_send.at[k],
            recv_sem=b_recv.at[k],
            device_id=(ctx, to[k]),
            device_id_type=MESH,
        )

    for k in order:
        dispatch(k).start()
    recv[ctx, exp] = buf_ref[exp]
    fetch(PIECES // 2)
    row = lax.broadcasted_iota(jnp.int32, (exp_count * block, exp_count * block), 0)
    column = lax.broadcasted_iota(jnp.int32, (exp_count * block, exp_count * block), 1)
    span_bits = slots.bit_length() - 1
    split = jnp.where(
        column == (row & (slots - 1)) * PIECES + (row >> span_bits), 1.0, 0.0
    ).astype(jnp.bfloat16)
    merge = jnp.where(
        row == (column & (slots - 1)) * PIECES + (column >> span_bits), 1.0, 0.0
    ).astype(jnp.bfloat16)
    for p in pairs:
        for k in (p, p + 1):
            if k > 0:
                dispatch(k).wait_recv()
        for d in range(ctx_count - 1):
            forward(d, p).start()
        fetch(2)
    fetch(len(pending))

    def spread(which):
        packed = recv[which].reshape(exp_count * block, width)
        apart = jnp.dot(split, packed, preferred_element_type=jnp.float32).astype(jnp.bfloat16)
        at = pl.ds(pl.multiple_of(which * slots, slots), slots)
        for piece in range(PIECES):
            rows_in[piece, at, :] = apart[piece * slots : (piece + 1) * slots, :]

    spread(ctx)
    for d in range(ctx_count - 1):
        for p in pairs:
            forward(d, p).wait_recv()
        spread(senders[d])

    gate = None
    up = None
    for piece in range(PIECES):
        weights_in[piece].wait()
        weights_in[PIECES + piece].wait()
        span = slice(piece * width, (piece + 1) * width)
        rows = rows_in[piece]
        gate_part = jnp.dot(rows, gate_w[span, :], preferred_element_type=jnp.float32)
        up_part = jnp.dot(rows, up_w[span, :], preferred_element_type=jnp.float32)
        gate = gate_part if gate is None else gate + gate_part
        up = up_part if up is None else up + up_part
    inner = (gate / (1.0 + jnp.exp(-gate)) * up).astype(jnp.bfloat16)
    for piece in range(PIECES):
        weights_in[2 * PIECES + piece].wait()
        span = slice(piece * width, (piece + 1) * width)
        result = jnp.dot(inner, down_w[:, span], preferred_element_type=jnp.float32)
        rows_in[piece] = result.astype(jnp.bfloat16)

    for k in order:
        dispatch(k).wait_send()
    for d in range(ctx_count - 1):
        for p in pairs:
            forward(d, p).wait_send()

    def gather(which):
        at = pl.ds(pl.multiple_of(which * slots, slots), slots)
        apart = jnp.concatenate([rows_in[piece, at, :] for piece in range(PIECES)], axis=0)
        packed = jnp.dot(merge, apart, preferred_element_type=jnp.float32).astype(jnp.bfloat16)
        recv[which] = packed.reshape(exp_count, block, width)

    for d in range(ctx_count - 1):
        gather(others[d])
        for p in back_pairs:
            give_back(d, p).start()
    gather(ctx)
    for p in back_pairs:
        for d in range(ctx_count - 1):
            give_back(d, p).wait_recv()
        for k in (p, p + 1):
            total = recv[ctx, to[k]].astype(jnp.float32)
            for d in range(ctx_count - 1):
                total = total + ret_in[d, to[k]].astype(jnp.float32)
            if k == 0:
                back[exp] = total.astype(jnp.bfloat16)
            else:
                out_buf[to[k]] = total.astype(jnp.bfloat16)
                hand_in(k).start()
    for k in order:
        hand_in(k).wait_recv()
    packed = back[...].reshape(exp_count * block, width)
    taken = jnp.dot(pick_ref[...], packed, preferred_element_type=jnp.float32)
    out_ref[...] = taken.astype(jnp.bfloat16)
    for k in order:
        hand_in(k).wait_send()
    for d in range(ctx_count - 1):
        for p in pairs:
            give_back(d, p).wait_send()


def expert_call(ctx_count, exp_count, pick, stack, gate_weight, up_weight, down_weight):
    block = pick.shape[1] // exp_count
    width = stack.shape[1]
    model, hidden = gate_weight.shape[1:]
    slots = exp_count * block // PIECES
    vmem = pl.BlockSpec(memory_space=pltpu.VMEM)
    anywhere = pl.BlockSpec(memory_space=pl.ANY)
    dma = pltpu.SemaphoreType.DMA
    return pl.pallas_call(
        functools.partial(expert_kernel, ctx_count, exp_count),
        out_shape=jax.ShapeDtypeStruct((pick.shape[0], width), jnp.bfloat16),
        in_specs=[vmem, vmem, anywhere, anywhere, anywhere],
        out_specs=vmem,
        scratch_shapes=[
            pltpu.VMEM((exp_count, block, width), jnp.bfloat16),
            pltpu.VMEM((exp_count, block, width), jnp.bfloat16),
            pltpu.VMEM((model, hidden), jnp.bfloat16),
            pltpu.VMEM((model, hidden), jnp.bfloat16),
            pltpu.VMEM((hidden, model), jnp.bfloat16),
            pltpu.VMEM((ctx_count, exp_count, block, width), jnp.bfloat16),
            pltpu.VMEM((PIECES, ctx_count * slots, width), jnp.bfloat16),
            pltpu.VMEM((ctx_count - 1, exp_count, block, width), jnp.bfloat16),
            pltpu.VMEM((exp_count, block, width), jnp.bfloat16),
            dma((3, PIECES)),
            dma((exp_count,)),
            dma((exp_count,)),
            dma((ctx_count - 1, exp_count)),
            dma((ctx_count - 1, exp_count)),
            dma((ctx_count - 1, exp_count)),
            dma((ctx_count - 1, exp_count)),
            dma((exp_count,)),
            dma((exp_count,)),
        ],
        compiler_params=pltpu.CompilerParams(
            collective_id=1, has_side_effects=True, vmem_limit_bytes=62 << 20
        ),
    )(pick, stack, gate_weight, up_weight, down_weight)


def on_device(
    queries,
    prior_codes,
    fresh_codes,
    prior_powers,
    fresh_powers,
    block_mask,
    value_up,
    output_weight,
    residual,
    norm_gain,
    router,
    route_ids,
    gate_weight,
    up_weight,
    down_weight,
):
    ctx_count = lax.axis_size("ctx")
    exp_count = lax.axis_size("exp")
    ctx_index = lax.axis_index("ctx")
    rows_block, head_count, key_width = queries.shape
    prior_blocks = prior_powers.shape[0]
    own_blocks = prior_blocks + 1
    scales = power_two(jnp.concatenate([prior_powers, fresh_powers], axis=0))
    code_rows = jnp.concatenate([prior_codes, fresh_codes], axis=0)
    latent_t = (
        code_rows.T.astype(jnp.float32) * jnp.repeat(scales, rows_block)[None, :]
    ).astype(jnp.bfloat16)
    q_rows = queries.transpose(1, 0, 2).reshape(head_count * rows_block, key_width)

    mask_row = lax.dynamic_index_in_dim(block_mask, ctx_index, 0, keepdims=False)
    prior_mask = mask_row[: prior_blocks * ctx_count].reshape(ctx_count, prior_blocks)
    fresh_mask = mask_row[prior_blocks * ctx_count :].reshape(ctx_count, 1)
    live = jnp.concatenate([prior_mask, fresh_mask], axis=1) > 0
    position = jnp.arange(rows_block)
    is_fresh = jnp.arange(own_blocks)[None, :] == prior_blocks
    is_own = jnp.arange(ctx_count)[:, None] == ctx_index
    diagonal = jnp.logical_and(is_fresh, is_own)
    causal = position[:, None] >= position[None, :]
    later = jnp.logical_and(is_fresh, jnp.arange(ctx_count)[:, None] > ctx_index)
    live = jnp.logical_and(live, jnp.logical_not(later))
    allowed = jnp.logical_and(
        live[:, None, :, None],
        jnp.logical_or(jnp.logical_not(diagonal)[:, None, :, None], causal[None, :, None, :]),
    )
    mask = allowed.reshape(ctx_count, rows_block, own_blocks * rows_block).astype(jnp.float32)

    attention = attention_call(
        ctx_count, exp_count, q_rows, latent_t, mask, value_up, output_weight
    )
    hidden = (residual.astype(jnp.float32) + attention).astype(jnp.bfloat16)
    hidden_wide = hidden.astype(jnp.float32)
    normed = (
        hidden_wide
        * lax.rsqrt(jnp.mean(hidden_wide * hidden_wide, axis=1, keepdims=True) + 1e-06)
        * norm_gain.astype(jnp.float32)
    ).astype(jnp.bfloat16)
    expert_count = router.shape[1]
    token_count, route_count = route_ids.shape
    model_width = normed.shape[1]
    capacity = token_count * route_count * 2 // expert_count
    affinity = jax.nn.sigmoid(jnp.dot(normed, router, preferred_element_type=jnp.float32))
    route_hits = route_ids[:, :, None] == jnp.arange(expert_count)[None, None, :]
    chosen = jnp.sum(jnp.where(route_hits, affinity[:, None, :], 0.0), axis=2)
    gate_values = 2.5 * chosen / jnp.sum(chosen, axis=1, keepdims=True)
    flat_hits = route_hits.reshape(token_count * route_count, expert_count).astype(jnp.int32)
    before = jnp.cumsum(flat_hits, axis=0) - flat_hits
    slot_index = jnp.sum(before * flat_hits, axis=1)
    target = (route_ids.reshape(-1) * capacity + slot_index).reshape(token_count, route_count)
    place = target.T[:, None, :] * PIECES + jnp.arange(PIECES)[None, :, None]
    pick = (
        place.reshape(-1)[:, None] == jnp.arange(expert_count * capacity * PIECES)[None, :]
    ).astype(jnp.bfloat16)
    width = model_width // PIECES
    stack = normed.reshape(token_count, PIECES, width).transpose(1, 0, 2)
    taken = expert_call(
        ctx_count,
        exp_count,
        pick,
        stack.reshape(PIECES * token_count, width),
        gate_weight,
        up_weight,
        down_weight,
    ).reshape(route_count, PIECES, token_count, width)
    gates = gate_values.T[:, None, :, None]
    expert_mix = jnp.sum(gates * taken.astype(jnp.float32), axis=0)
    expert_mix = expert_mix.transpose(1, 0, 2).reshape(token_count, model_width)
    return (hidden_wide + expert_mix).astype(jnp.bfloat16)


def solution(mesh):
    in_specs = (
        P("ctx", "exp", None),
        P("ctx", None),
        P("ctx", None),
        P("ctx"),
        P("ctx"),
        P(),
        P("exp", None, None),
        P("exp", None),
        P(("ctx", "exp"), None),
        P(),
        P(),
        P(("ctx", "exp"), None),
        P("exp", None, "ctx"),
        P("exp", None, "ctx"),
        P("exp", "ctx", None),
    )
    out_specs = P(("ctx", "exp"), None)
    return jax.shard_map(
        on_device, mesh=mesh, in_specs=in_specs, out_specs=out_specs, check_vma=False
    )
```
